256 devices in a mesh: grp: 16 (over z, core), dev: 16 (over x, y).
Axes of the slice: x: 4, y: 4, z: 8, core: 2. Of those that a mesh axis runs over, the one named last changes fastest.
Arguments:
- fields: float32 [6, 64, 32, 32, 128], P(None, None, 'grp', 'dev'), may hold values from 0.14 to 7
- speeds: float32 [3, 2, 32, 32, 128], P(None, None, 'grp', 'dev'), may hold values from -1.5 to 1.5, as said below
- sharpen: float32 [64, 64], replicated, may hold values from -0.75 to 0.75
- mat_count: int32 [32, 32, 128], P('grp', 'dev'), may hold values from 1 to 6, as said below
Outputs:
- remapped: float32 [6, 64, 32, 32, 128], P(None, None, 'grp', 'dev')
The draws below stay inside these ranges and needn't reach their ends.
Inputs may be any that keep to these rules, and one draw needn't show every extreme that they name: `speeds`: the upper-face speed of an element along a direction equals the lower-face speed of the next element along it, periodically. `mat_count`: an element with 2 or more materials is mixed.
All inputs are finite; a program needn't handle non-finite values.
Results may differ from the reference program's by a relative error of at most 0.0001.
Values sent between devices are 32-bit elements; how exact they have to be, the bound alone decides.
No kernel may reach another device: no remote copies, remote signals or barrier semaphores. Data moves between devices by JAX's collectives and lax.ppermute only.
A program may use at most 64 MiB of HBM per device.

```python
import math
import jax
import jax.numpy as jnp
import numpy as np
from jax import lax

FIELDS = 6
NODES = 64
CX = 128
CY = 2
CZ = 2
CAP = 256
NX = 128
NY = 32
NZ = 32


def draw_fields(key, part):
    key = jax.random.fold_in(key, 5)
    wave_key, phase_key, rough_key, width_key, node_key = jax.random.split(key, 5)
    waves = jax.random.randint(wave_key, (3, FIELDS, 3), 1, 4).astype(jnp.float32)
    phases = jax.random.uniform(phase_key, (3, FIELDS), jnp.float32, -math.pi, math.pi)
    depth = jnp.arange(NZ, dtype=jnp.float32)[None, :, None, None] / NZ
    rows = jnp.arange(NY, dtype=jnp.float32)[None, None, :, None] / NY
    cols = jnp.arange(NX, dtype=jnp.float32)[None, None, None, :] / NX
    smooth = jnp.zeros((FIELDS, NZ, NY, NX), jnp.float32)
    for term in range(3):
        angle = 2.0 * math.pi * (waves[term, :, 0][:, None, None, None] * cols + waves[term, :, 1][:, None, None, None] * rows + waves[term, :, 2][:, None, None, None] * depth)
        smooth = smooth + 0.3 * jnp.sin(angle + phases[term][:, None, None, None])
    rough = jax.random.uniform(rough_key, (FIELDS, NZ, NY, NX), jnp.float32, -0.4, 0.4)
    spread = jnp.exp(jax.random.uniform(width_key, (FIELDS, NZ, NY, NX), jnp.float32, math.log(0.1), math.log(0.6)))
    shape_u = jnp.tanh(jax.random.normal(node_key, (FIELDS, NODES, NZ, NY, NX), jnp.float32))
    log_value = (smooth + rough)[:, None] + spread[:, None] * shape_u
    return jnp.exp(log_value).astype(jnp.float32)


def draw_speeds(key, part):
    key = jax.random.fold_in(key, 11)
    base = jnp.clip(0.6 * jax.random.normal(key, (3, NZ, NY, NX), jnp.float32), -1.5, 1.5)
    upper = jnp.stack([jnp.roll(base[0], -1, 2), jnp.roll(base[1], -1, 1), jnp.roll(base[2], -1, 0)])
    return jnp.stack([base, upper], axis=1)


def draw_mat_count(key, part):
    key = jax.random.fold_in(key, 23)
    groups = NZ // CZ
    members = NY // CY
    cells = CZ * CY * CX
    hot_key, pick_key, cold_key, place_key, level_key = jax.random.split(key, 5)
    hot = jax.random.randint(hot_key, (), 0, groups)
    chosen = jax.random.randint(pick_key, (), 0, members)
    cold = jax.random.randint(cold_key, (groups, members), CAP // 8, 3 * CAP // 8 + 1)
    remaining = CAP * members // 2 - CAP
    index = jnp.arange(members, dtype=jnp.int32)
    rank = index - (index > chosen).astype(jnp.int32)
    share = remaining // (members - 1) + (rank < remaining % (members - 1)).astype(jnp.int32)
    hot_row = jnp.where(index == chosen, CAP, share)
    is_hot = jnp.arange(groups, dtype=jnp.int32)[:, None] == hot
    loads = jnp.where(is_hot, hot_row[None, :], cold).reshape(-1)
    device_keys = jax.random.split(place_key, groups * members)

    def ranks_of(device_key):
        order = jax.random.permutation(device_key, cells)
        return jnp.zeros((cells,), jnp.int32).at[order].set(jnp.arange(cells, dtype=jnp.int32))
    ranks = jax.vmap(ranks_of)(device_keys)
    flags = ranks < loads[:, None]
    levels = jax.random.randint(level_key, (groups * members, cells), 2, 7)
    counts = jnp.where(flags, levels, 1)
    counts = counts.reshape(groups, members, CZ, CY, CX).transpose(0, 2, 1, 3, 4).reshape(NZ, NY, NX)
    return counts.astype(jnp.int32)


def bell_draw(key, extent, scale, bound, kind=jnp.bfloat16):
    drawn = jax.random.normal(key, extent, jnp.float32) * scale
    return jnp.minimum(jnp.maximum(drawn, -bound), bound).astype(kind)


def setup_inputs(seed: int = 0) -> dict:
    splits = jax.random.split(jax.random.key(seed), 5)
    fields = draw_fields(jax.random.fold_in(splits[4], 71), 0)
    speeds = draw_speeds(jax.random.fold_in(splits[4], 71), 0)
    sharpen = bell_draw(splits[2], (NODES, NODES), NODES ** -0.5, 0.75, jnp.float32)
    mat_count = draw_mat_count(jax.random.fold_in(splits[4], 71), 0)
    return {"fields": fields, "speeds": speeds, "sharpen": sharpen, "mat_count": mat_count}


DT = 0.08
LIFT = 6.0

def gll_derivative():
    points = np.array([-1.0, -1.0 / np.sqrt(5.0), 1.0 / np.sqrt(5.0), 1.0])
    products = np.array([np.prod([points[first] - points[second] for second in range(4) if second != first]) for first in range(4)])
    matrix = np.zeros((4, 4))
    for first in range(4):
        for second in range(4):
            if first != second:
                matrix[first, second] = products[first] / products[second] / (points[first] - points[second])
        matrix[first, first] = sum((1.0 / (points[first] - points[other]) for other in range(4) if other != first))
    return matrix

def node_tables():
    small = gll_derivative()
    along_x = np.kron(np.eye(16), small)
    along_y = np.kron(np.kron(np.eye(4), small), np.eye(4))
    along_z = np.kron(small, np.eye(16))
    return np.stack([along_x, along_y, along_z]).astype(np.float32)

def face_terms(nodal, shaped, node_axis, plus_high, plus_low, speed_low, speed_high, center):
    low_index = [slice(None)] * nodal.ndim
    high_index = [slice(None)] * nodal.ndim
    low_index[node_axis] = 0
    high_index[node_axis] = 3
    lower = shaped[tuple(low_index)]
    upper = shaped[tuple(high_index)]
    term_high = jnp.maximum(speed_high, 0.0) * upper + jnp.minimum(speed_high, 0.0) * plus_high - center * upper
    term_low = center * lower - jnp.maximum(speed_low, 0.0) * plus_low - jnp.minimum(speed_low, 0.0) * lower
    nodal = nodal.at[tuple(high_index)].add(-LIFT * term_high)
    return nodal.at[tuple(low_index)].add(-LIFT * term_low)

def tendency_one(field, speeds, tables):
    flat = field.reshape(NODES, -1)
    total = jnp.zeros_like(flat)
    for direction in range(3):
        center = 0.5 * (speeds[direction, 0] + speeds[direction, 1])
        slope = jnp.dot(tables[direction], flat, precision=lax.Precision.HIGHEST)
        total = total - center.reshape(-1) * slope
    nodal = total.reshape(4, 4, 4, NZ, NY, NX)
    shaped = field.reshape(4, 4, 4, NZ, NY, NX)
    for direction in range(3):
        node_axis = 2 - direction
        lower = jnp.take(shaped, 0, axis=node_axis)
        upper = jnp.take(shaped, 3, axis=node_axis)
        plus_high = jnp.roll(lower, -1, axis=4 - direction)
        plus_low = jnp.roll(upper, 1, axis=4 - direction)
        center = 0.5 * (speeds[direction, 0] + speeds[direction, 1])
        nodal = face_terms(nodal, shaped, node_axis, plus_high, plus_low, speeds[direction, 0], speeds[direction, 1], center)
    return nodal.reshape(field.shape)

def neighbour_bounds(field):
    highest = lax.optimization_barrier(jnp.max(field, axis=0))
    lowest = lax.optimization_barrier(jnp.min(field, axis=0))
    upper = highest
    lower = lowest
    for axis_number in range(3):
        upper = jnp.maximum(upper, jnp.maximum(jnp.roll(highest, 1, axis_number), jnp.roll(highest, -1, axis_number)))
        lower = jnp.minimum(lower, jnp.minimum(jnp.roll(lowest, 1, axis_number), jnp.roll(lowest, -1, axis_number)))
    return (upper, lower)

def material_fix(block, counts, sharpen):
    present = (jnp.arange(FIELDS, dtype=jnp.float32)[:, None] < counts[None, :]).astype(jnp.float32)
    average = lax.optimization_barrier(jnp.sum(block * present[:, None, :], axis=0)) / counts[None, :]
    offsets = (block - average[None]) * present[:, None, :]
    return jnp.einsum('mn,fns->fms', sharpen, offsets, precision=lax.Precision.HIGHEST)

def reference(fields, speeds, sharpen, mat_count):
    tables = jnp.asarray(node_tables())

    def one_field(field):
        upper, lower = neighbour_bounds(field)
        section_one = field + DT * tendency_one(field, speeds, tables)
        section_two = 0.75 * field + 0.25 * (section_one + DT * tendency_one(section_one, speeds, tables))
        section_three = field / 3.0 + 2.0 / 3.0 * (section_two + DT * tendency_one(section_two, speeds, tables))
        return (section_three, upper, lower)
    advected, upper, lower = lax.map(one_field, fields)
    flat = advected.reshape(FIELDS, NODES, -1)
    counts = mat_count.reshape(-1).astype(jnp.float32)
    sharpened = (flat + material_fix(flat, counts, sharpen)).reshape(fields.shape)
    return jnp.minimum(jnp.maximum(sharpened, lower[:, None]), upper[:, None])
```

```python
import functools

import jax
import jax.numpy as jnp
import numpy as np
from jax import lax
from jax.experimental import pallas as pl
from jax.experimental.pallas import tpu as pltpu
from jax.sharding import PartitionSpec as P

DT = 0.08
LIFT = 6.0
NODE = (3, 4, 4, 4, 8, 128)
ROW = (6, 32, 8, 128)
FACE = 24
EXT = 3
STEP = {"dev": 1, "grp": 2}
LIMIT = 48 * 1024 * 1024


def gll_derivative():
    points = np.array([-1.0, -1.0 / np.sqrt(5.0), 1.0 / np.sqrt(5.0), 1.0])
    products = np.array(
        [
            np.prod([points[first] - points[second] for second in range(4) if second != first])
            for first in range(4)
        ]
    )
    matrix = np.zeros((4, 4))
    for first in range(4):
        for second in range(4):
            if first != second:
                matrix[first, second] = (
                    products[first] / products[second] / (points[first] - points[second])
                )
        matrix[first, first] = sum(
            (1.0 / (points[first] - points[other]) for other in range(4) if other != first)
        )
    return matrix


D = gll_derivative()
EVEN = [float(D[r, 0] + D[r, 3]) / 2 for r in (0, 1)]
ODD = [(float(D[r, 0] - D[r, 3]) / 2, float(D[r, 1] - D[r, 2]) / 2) for r in (0, 1)]


def roll(x, shift, axis):
    size = x.shape[axis]
    return pltpu.roll(x, shift % size, axis)


def sublane(shape):
    return lax.broadcasted_iota(jnp.int32, shape, len(shape) - 2)


def bit(shape, step):
    return (sublane(shape) & step) != 0


def even_device(axis):
    return lax.rem(lax.axis_index(axis), 2) == 0


def coefficients(speeds_ref):
    out = []
    low_half = sublane((8, 128)) < 4
    for d in range(3):
        v = speeds_ref[pl.ds(8 * d, 8), :]
        w = roll(v, 4, 0)
        a = jnp.where(low_half, v, w)
        b = jnp.where(low_half, w, v)
        c = 0.5 * (a + b)
        out.append(
            (
                -DT * c,
                (-DT * LIFT) * (c - jnp.minimum(a, 0.0)),
                (DT * LIFT) * jnp.maximum(a, 0.0),
                (-DT * LIFT) * (jnp.maximum(b, 0.0) - c),
                (-DT * LIFT) * jnp.minimum(b, 0.0),
            )
        )
    return out


def line(q, c):
    t = c * ((q[0] + q[3]) - (q[1] + q[2]))
    o0 = c * (q[0] - q[3])
    o1 = c * (q[1] - q[2])
    e = [EVEN[r] * t for r in (0, 1)]
    o = [ODD[r][0] * o0 + ODD[r][1] * o1 for r in (0, 1)]
    return [e[0] + o[0], e[1] + o[1], o[1] - e[1], o[0] - e[0]]


def with_faces(q, coef, dn, up):
    c, low, low_in, high, high_in = coef
    r = line(q, c)
    r[0] = r[0] + (low * q[0] + low_in * dn)
    r[3] = r[3] + (high * q[3] + high_in * up)
    return r


def beside(low, high, halo_dn, halo_up, step):
    upper = bit(low.shape, step)
    dn = jnp.where(upper, roll(high, step, low.ndim - 2), halo_dn)
    up = jnp.where(upper, halo_up, roll(low, -step, low.ndim - 2))
    return dn, up


def pack_high(a, b, step):
    return jnp.where(bit(a.shape, step), b, roll(a, -step, a.ndim - 2))


def pack_low(a, b, step):
    return jnp.where(bit(a.shape, step), roll(a, step, a.ndim - 2), b)


def unpack_dn(m, second, step):
    return roll(m, -step, m.ndim - 2) if second else m


def unpack_up(m, second, step):
    return roll(m, step, m.ndim - 2) if second else m


def tendency(q_ref, acc_ref, p, coef, halo_y, halo_z, finish):
    for k in range(4):
        qx = [q_ref[p, k, :, i] for i in range(4)]
        rx = with_faces(qx, coef[0], roll(qx[3], 1, 2), roll(qx[0], -1, 2))
        for i in range(4):
            acc_ref[p, k, :, i] = rx[i]
        qy = [q_ref[p, k, j] for j in range(4)]
        dn, up = beside(qy[0], qy[3], *halo_y(p, k), 1)
        ry = with_faces(qy, coef[1], dn, up)
        for j in range(4):
            acc_ref[p, k, j] = acc_ref[p, k, j] + ry[j]
    for j in range(4):
        qz = [q_ref[p, k, j] for k in range(4)]
        dn, up = beside(qz[0], qz[3], *halo_z(p, j), 2)
        rz = with_faces(qz, coef[2], dn, up)
        for k in range(4):
            finish(p, k, j, qz[k], acc_ref[p, k, j] + rz[k])


def put_messages(q_ref, p, messages):
    outs = {"dev": messages[:2], "grp": messages[2:]}
    for axis in ("dev", "grp"):
        step = STEP[axis]
        even = even_device(axis)
        first, second = outs[axis]
        for half in range(2):
            m = 2 * half
            if axis == "dev":
                low = [q_ref[p, m, 0], q_ref[p, m + 1, 0]]
                high = [q_ref[p, m, 3], q_ref[p, m + 1, 3]]
            else:
                low = [q_ref[p, 0, m], q_ref[p, 0, m + 1]]
                high = [q_ref[p, 3, m], q_ref[p, 3, m + 1]]
            to_next = pack_high(high[0], high[1], step)
            to_last = pack_low(low[0], low[1], step)
            at = pl.ds(8 * p + 4 * half, 4)
            first[at] = jnp.where(even, to_next, to_last)
            second[at] = jnp.where(even, to_last, to_next)


def halo_reader(first, second, axis):
    step = STEP[axis]
    even = even_device(axis)

    def read(p, plane):
        at = pl.ds(8 * p + 4 * (plane // 2), 4)
        x, y = first[at], second[at]
        dn = unpack_dn(jnp.where(even, y, x), plane % 2, step)
        up = unpack_up(jnp.where(even, x, y), plane % 2, step)
        return dn, up

    return read


def open_kernel(fields_ref, q_ref, ext_ref, *messages):
    low_half = sublane((8, 128)) < 4

    def pair(p, carry):
        tops, bottoms = [], []
        for k in range(4):
            for j in range(4):
                for h in range(2):
                    m = 8 * k + 2 * j + h
                    a = fields_ref[2 * p, m]
                    b = fields_ref[2 * p + 1, m]
                    x = jnp.where(low_half, a, roll(b, 4, 0))
                    y = jnp.where(low_half, roll(a, 4, 0), b)
                    q_ref[p, k, j, 2 * h] = x
                    q_ref[p, k, j, 2 * h + 1] = y
                    tops.append(jnp.maximum(x, y))
                    bottoms.append(jnp.minimum(x, y))
        while len(tops) > 1:
            tops = [jnp.maximum(x, y) for x, y in zip(tops[::2], tops[1::2])]
            bottoms = [jnp.minimum(x, y) for x, y in zip(bottoms[::2], bottoms[1::2])]
        ext_ref[0, p] = tops[0]
        ext_ref[1, p] = bottoms[0]
        put_messages(q_ref, p, messages)
        outs = {"dev": messages[:2], "grp": messages[2:]}
        for axis in ("dev", "grp"):
            even = even_device(axis)
            to_next = pack_high(tops[0], bottoms[0], STEP[axis])
            to_last = pack_low(tops[0], bottoms[0], STEP[axis])
            first, second = outs[axis]
            first[FACE + p] = jnp.where(even, to_next, to_last)
            second[FACE + p] = jnp.where(even, to_last, to_next)
        return carry

    lax.fori_loop(0, 3, pair, 0)


def bounds(ext_ref, messages, p):
    top, bottom = ext_ref[0, p], ext_ref[1, p]
    upper = jnp.maximum(top, jnp.maximum(roll(top, 1, 1), roll(top, -1, 1)))
    lower = jnp.minimum(bottom, jnp.minimum(roll(bottom, 1, 1), roll(bottom, -1, 1)))
    outs = {"dev": messages[:2], "grp": messages[2:]}
    for axis in ("dev", "grp"):
        step = STEP[axis]
        even = even_device(axis)
        first, second = outs[axis]
        x, y = first[FACE + p], second[FACE + p]
        from_last = jnp.where(even, y, x)
        from_next = jnp.where(even, x, y)
        for second_half, combine in ((0, jnp.maximum), (1, jnp.minimum)):
            own = (top, bottom)[second_half]
            dn, up = beside(
                own,
                own,
                unpack_dn(from_last, second_half, step),
                unpack_up(from_next, second_half, step),
                step,
            )
            if second_half == 0:
                upper = jnp.maximum(upper, jnp.maximum(dn, up))
            else:
                lower = jnp.minimum(lower, jnp.minimum(dn, up))
    return upper, lower


def first_kernel(q_ref, speeds_ref, ext_ref, *refs):
    got, (s_ref, limit_ref), messages = refs[:4], refs[4:6], refs[6:]
    coef = coefficients(speeds_ref)
    halo_y = halo_reader(got[0], got[1], "dev")
    halo_z = halo_reader(got[2], got[3], "grp")

    def finish(p, k, j, q, t):
        s_ref[p, k, j] = q + t

    def pair(p, carry):
        tendency(q_ref, s_ref, p, coef, halo_y, halo_z, finish)
        put_messages(s_ref, p, messages)
        upper, lower = bounds(ext_ref, got, p)
        limit_ref[0, p] = upper
        limit_ref[1, p] = lower
        return carry

    lax.fori_loop(0, 3, pair, 0)


def second_kernel(q_ref, s_ref, speeds_ref, *refs):
    got, out_ref, messages = refs[:4], refs[4], refs[5:]
    coef = coefficients(speeds_ref)
    halo_y = halo_reader(got[0], got[1], "dev")
    halo_z = halo_reader(got[2], got[3], "grp")

    def finish(p, k, j, s, t):
        out_ref[p, k, j] = 0.75 * q_ref[p, k, j] + 0.25 * (s + t)

    def pair(p, carry):
        tendency(s_ref, out_ref, p, coef, halo_y, halo_z, finish)
        put_messages(out_ref, p, messages)
        return carry

    lax.fori_loop(0, 3, pair, 0)


def operator_kernel(sharpen_ref, high_ref, low_ref):
    s = sharpen_ref[...]
    high = s.astype(jnp.bfloat16)
    low = (s - high.astype(jnp.float32)).astype(jnp.bfloat16)
    rows = lax.broadcasted_iota(jnp.int32, (256, 64), 0)
    cols = lax.broadcasted_iota(jnp.int32, (256, 64), 1)
    tall = (rows // 4 == cols).astype(jnp.bfloat16)
    rows = lax.broadcasted_iota(jnp.int32, (64, 256), 0)
    cols = lax.broadcasted_iota(jnp.int32, (64, 256), 1)
    wide = (cols // 4 == rows).astype(jnp.bfloat16)
    rows = lax.broadcasted_iota(jnp.int32, (256, 256), 0)
    cols = lax.broadcasted_iota(jnp.int32, (256, 256), 1)
    same = (rows & 3) == (cols & 3)
    for part, ref in ((high, high_ref), (low, low_ref)):
        half = jnp.dot(tall, part, preferred_element_type=jnp.float32).astype(jnp.bfloat16)
        full = jnp.dot(half, wide, preferred_element_type=jnp.float32)
        ref[...] = jnp.where(same, full, 0.0).astype(jnp.bfloat16)


def last_kernel(q_ref, s_ref, speeds_ref, limit_ref, count_ref, high_ref, low_ref, *refs):
    got, out_ref, acc_ref, off_ref = refs[:4], refs[4], refs[5], refs[6]
    coef = coefficients(speeds_ref)
    halo_y = halo_reader(got[0], got[1], "dev")
    halo_z = halo_reader(got[2], got[3], "grp")
    low_half = sublane((8, 128)) < 4

    def finish(p, k, j, s, t):
        acc_ref[p, k, j] = q_ref[p, k, j] * (1.0 / 3.0) + (2.0 / 3.0) * (s + t)

    def pair(p, carry):
        tendency(s_ref, acc_ref, p, coef, halo_y, halo_z, finish)
        return carry

    lax.fori_loop(0, 3, pair, 0)

    counts = count_ref[...].astype(jnp.float32)
    counts = jnp.concatenate([counts, counts], axis=0)
    present = [(counts > float(f)).astype(jnp.float32) for f in range(6)]
    share = 1.0 / counts

    def node_pair(k, carry):
        for j in range(4):
            for h in range(2):
                m = 8 * k + 2 * j + h
                rows = []
                for p in range(3):
                    x = acc_ref[p, k, j, 2 * h]
                    y = acc_ref[p, k, j, 2 * h + 1]
                    rows.append(jnp.where(low_half, x, roll(y, 4, 0)))
                    rows.append(jnp.where(low_half, roll(x, 4, 0), y))
                mean = rows[0] * present[0]
                for f in range(1, 6):
                    mean = mean + rows[f] * present[f]
                mean = mean * share
                for f in range(6):
                    out_ref[f, m] = rows[f]
                    off_ref[f, m] = (rows[f] - mean) * present[f]
        return carry

    lax.fori_loop(0, 4, node_pair, 0)

    high, low = high_ref[...], low_ref[...]
    for p in range(3):
        off = jnp.concatenate(
            [off_ref[2 * p].reshape(256, 128), off_ref[2 * p + 1].reshape(256, 128)], axis=1
        )
        off_high = off.astype(jnp.bfloat16)
        off_low = (off - off_high.astype(jnp.float32)).astype(jnp.bfloat16)
        fix = jnp.dot(high, off_high, preferred_element_type=jnp.float32)
        fix = fix + jnp.dot(high, off_low, preferred_element_type=jnp.float32)
        fix = fix + jnp.dot(low, off_high, preferred_element_type=jnp.float32)
        upper, lower = limit_ref[0, p], limit_ref[1, p]
        for h in range(2):
            u, v = roll(upper, 4, 0), roll(lower, 4, 0)
            if h == 0:
                u, v = jnp.where(low_half, upper, u), jnp.where(low_half, lower, v)
            else:
                u, v = jnp.where(low_half, u, upper), jnp.where(low_half, v, lower)
            f = 2 * p + h
            value = out_ref[f] + fix[:, 128 * h : 128 * h + 128].reshape(32, 8, 128)
            out_ref[f] = jnp.minimum(jnp.maximum(value, v), u)


def call(kernel, outs, args, scratch=(), flops=5_000_000):
    return pl.pallas_call(
        kernel,
        out_shape=[jax.ShapeDtypeStruct(*o) for o in outs],
        in_specs=[pl.BlockSpec(memory_space=pltpu.VMEM)] * len(args),
        out_specs=[pl.BlockSpec(memory_space=pltpu.VMEM)] * len(outs),
        scratch_shapes=[pltpu.VMEM(*s) for s in scratch],
        compiler_params=pltpu.CompilerParams(vmem_limit_bytes=LIMIT),
        cost_estimate=pl.CostEstimate(flops=flops, bytes_accessed=2_000_000, transcendentals=0),
    )(*args)


EVEN_PAIRS = [(i, i ^ 1) for i in range(16)]
ODD_PAIRS = [((i + 1) % 16, ((i ^ 1) + 1) % 16) for i in range(16)]


def exchange(messages):
    ways = (("dev", EVEN_PAIRS), ("dev", ODD_PAIRS), ("grp", EVEN_PAIRS), ("grp", ODD_PAIRS))
    return [lax.ppermute(m, axis, pairs) for m, (axis, pairs) in zip(messages, ways)]


def shards(fields, speeds, sharpen, mat_count):
    f32, bf16 = jnp.float32, jnp.bfloat16
    rows = fields.reshape(ROW)
    speeds = speeds.reshape(24, 128)
    counts = mat_count.reshape(4, 128)
    face = ((FACE, 8, 128), f32)
    face_ext = ((FACE + EXT, 8, 128), f32)
    ext = ((2, 3, 8, 128), f32)
    high, low = call(operator_kernel, [((256, 256), bf16)] * 2, [sharpen])
    q, extremes, *messages = call(open_kernel, [(NODE, f32), ext] + [face_ext] * 4, [rows])
    got = exchange(messages)
    s, limits, *messages = call(
        first_kernel, [(NODE, f32), ext] + [face] * 4, [q, speeds, extremes, *got]
    )
    got = exchange(messages)
    s, *messages = call(second_kernel, [(NODE, f32)] + [face] * 4, [q, s, speeds, *got])
    got = exchange(messages)
    (out,) = call(
        last_kernel,
        [(ROW, f32)],
        [q, s, speeds, limits, counts, high, low, *got],
        scratch=[(NODE, f32), (ROW, f32)],
    )
    return out.reshape(fields.shape)


def solution(mesh):
    in_specs = (
        P(None, None, "grp", "dev", None),
        P(None, None, "grp", "dev", None),
        P(),
        P("grp", "dev", None),
    )
    out_specs = P(None, None, "grp", "dev", None)
    return jax.shard_map(shards, mesh=mesh, in_specs=in_specs, out_specs=out_specs, check_vma=False)
```

```python
import functools

import jax
import jax.numpy as jnp
import numpy as np
from jax import lax
from jax.experimental import pallas as pl
from jax.experimental.pallas import tpu as pltpu
from jax.sharding import PartitionSpec as P

DT = 0.08
LIFT = 6.0
NODE = (3, 4, 4, 4, 8, 128)
ROW = (6, 32, 8, 128)
FACE = 24
EXT = 2 * FACE
COEF = EXT + 3
STEP = {"dev": 1, "grp": 2}
LIMIT = 48 * 1024 * 1024


def gll_derivative():
    points = np.array([-1.0, -1.0 / np.sqrt(5.0), 1.0 / np.sqrt(5.0), 1.0])
    products = np.array(
        [
            np.prod([points[first] - points[second] for second in range(4) if second != first])
            for first in range(4)
        ]
    )
    matrix = np.zeros((4, 4))
    for first in range(4):
        for second in range(4):
            if first != second:
                matrix[first, second] = (
                    products[first] / products[second] / (points[first] - points[second])
                )
        matrix[first, first] = sum(
            (1.0 / (points[first] - points[other]) for other in range(4) if other != first)
        )
    return matrix


D = gll_derivative()
EVEN = [float(D[r, 0] + D[r, 3]) / 2 for r in (0, 1)]
ODD = [(float(D[r, 0] - D[r, 3]) / 2, float(D[r, 1] - D[r, 2]) / 2) for r in (0, 1)]


def roll(x, shift, axis):
    size = x.shape[axis]
    return pltpu.roll(x, shift % size, axis)


def sublane(shape):
    return lax.broadcasted_iota(jnp.int32, shape, len(shape) - 2)


def bit(shape, step):
    return (sublane(shape) & step) != 0


def even_device(axis):
    return lax.rem(lax.axis_index(axis), 2) == 0


def coefficients(speeds_ref):
    out = []
    low_half = sublane((8, 128)) < 4
    for d in range(3):
        v = speeds_ref[pl.ds(8 * d, 8), :]
        w = roll(v, 4, 0)
        a = jnp.where(low_half, v, w)
        b = jnp.where(low_half, w, v)
        c = 0.5 * (a + b)
        out.append(
            (
                -DT * c,
                (-DT * LIFT) * (c - jnp.minimum(a, 0.0)),
                (DT * LIFT) * jnp.maximum(a, 0.0),
                (-DT * LIFT) * (jnp.maximum(b, 0.0) - c),
                (-DT * LIFT) * jnp.minimum(b, 0.0),
                (-DT * LIFT) * jnp.minimum(a, 0.0),
                (DT * LIFT) * jnp.maximum(b, 0.0),
            )
        )
    return out


def rim_coefficients(coef, step):
    upper = bit((8, 128), step)
    return jnp.where(upper, coef[4], coef[2]), jnp.where(upper, coef[6], coef[5])


def line(q, c):
    t = c * ((q[0] + q[3]) - (q[1] + q[2]))
    o0 = c * (q[0] - q[3])
    o1 = c * (q[1] - q[2])
    e = [EVEN[r] * t for r in (0, 1)]
    o = [ODD[r][0] * o0 + ODD[r][1] * o1 for r in (0, 1)]
    return [e[0] + o[0], e[1] + o[1], o[1] - e[1], o[0] - e[0]]


def with_faces(q, coef, dn, up):
    c, low, low_in, high, high_in = coef[:5]
    r = line(q, c)
    r[0] = r[0] + (low * q[0] + low_in * dn)
    r[3] = r[3] + (high * q[3] + high_in * up)
    return r


def beside(low, high, halo_dn, halo_up, step):
    upper = bit(low.shape, step)
    dn = jnp.where(upper, roll(high, step, low.ndim - 2), halo_dn)
    up = jnp.where(upper, halo_up, roll(low, -step, low.ndim - 2))
    return dn, up


def pack_high(a, b, step):
    return jnp.where(bit(a.shape, step), b, roll(a, -step, a.ndim - 2))


def pack_low(a, b, step):
    return jnp.where(bit(a.shape, step), roll(a, step, a.ndim - 2), b)


def unpack_dn(m, second, step):
    return roll(m, -step, m.ndim - 2) if second else m


def unpack_up(m, second, step):
    return roll(m, step, m.ndim - 2) if second else m


def tendency(q_ref, acc_ref, p, coef, halo_y, halo_z, finish):
    for k in range(4):
        qx = [q_ref[p, k, :, i] for i in range(4)]
        rx = with_faces(qx, coef[0], roll(qx[3], 1, 2), roll(qx[0], -1, 2))
        for i in range(4):
            acc_ref[p, k, :, i] = rx[i]
        qy = [q_ref[p, k, j] for j in range(4)]
        dn, up = beside(qy[0], qy[3], *halo_y(p, k), 1)
        ry = with_faces(qy, coef[1], dn, up)
        for j in range(4):
            acc_ref[p, k, j] = acc_ref[p, k, j] + ry[j]
    for j in range(4):
        qz = [q_ref[p, k, j] for k in range(4)]
        dn, up = beside(qz[0], qz[3], *halo_z(p, j), 2)
        rz = with_faces(qz, coef[2], dn, up)
        for k in range(4):
            finish(p, k, j, qz[k], acc_ref[p, k, j] + rz[k])


AXES = ("dev", "grp")


def put(messages, axis, at, to_next, to_last):
    even = even_device(axis)
    second, first = messages[2 * AXES.index(axis) :][:2]
    first[at] = jnp.where(even, to_next, to_last)
    second[at] = jnp.where(even, to_last, to_next)


def get(messages, axis, at):
    even = even_device(axis)
    second, first = messages[2 * AXES.index(axis) :][:2]
    x, y = first[at], second[at]
    return jnp.where(even, y, x), jnp.where(even, x, y)


def get_single(messages, axis, at, second):
    last, after = get(messages, axis, at)
    step = STEP[axis]
    return unpack_dn(last, second, step), unpack_up(after, second, step)


def face(q_ref, p, axis, side, plane):
    return q_ref[p, plane, side] if axis == "dev" else q_ref[p, side, plane]


def put_faces(q_ref, p, messages, base):
    for axis in AXES:
        step = STEP[axis]
        for half in range(2):
            m = 2 * half
            low = [face(q_ref, p, axis, 0, m + h) for h in range(2)]
            high = [face(q_ref, p, axis, 3, m + h) for h in range(2)]
            put(
                messages,
                axis,
                pl.ds(base + 8 * p + 4 * half, 4),
                pack_high(high[0], high[1], step),
                pack_low(low[0], low[1], step),
            )


def get_face(messages, axis, p, plane, base):
    at = pl.ds(base + 8 * p + 4 * (plane // 2), 4)
    return get_single(messages, axis, at, plane % 2)


def no_halo(p, plane):
    zero = jnp.zeros((4, 8, 128), jnp.float32)
    return zero, zero


def open_kernel(fields_hbm, speeds_hbm, count_hbm, *refs):
    q_ref, s_ref, ext_ref, wide_count_ref, speeds_ref = refs[:5]
    messages, (fields_ref, count_ref, sems) = refs[5:9], refs[9:]
    copies = [
        pltpu.make_async_copy(speeds_hbm, speeds_ref, sems.at[3]),
        pltpu.make_async_copy(count_hbm, count_ref, sems.at[4]),
    ]

    def part(p):
        at = pl.ds(2 * p, 2)
        return pltpu.make_async_copy(fields_hbm.at[at], fields_ref.at[at], sems.at[p])

    for copy in copies + [part(p) for p in range(3)]:
        copy.start()
    for copy in copies:
        copy.wait()
    low_half = sublane((8, 128)) < 4
    coef = coefficients(speeds_ref)
    counts = count_ref[...].astype(jnp.float32)
    wide_count_ref[...] = jnp.concatenate([counts, counts], axis=0)
    for axis, d in (("dev", 2), ("grp", 1)):
        pair = rim_coefficients(coef[d], STEP[AXES[d - 1]])
        put(
            messages,
            axis,
            COEF,
            pack_high(pair[0], pair[1], STEP[axis]),
            pack_low(pair[0], pair[1], STEP[axis]),
        )

    def finish(p, k, j, q, t):
        s_ref[p, k, j] = q + t

    def pair(p, carry):
        part(p).wait()
        tops, bottoms = [], []
        for k in range(4):
            for j in range(4):
                for h in range(2):
                    m = 8 * k + 2 * j + h
                    a = fields_ref[2 * p, m]
                    b = fields_ref[2 * p + 1, m]
                    x = jnp.where(low_half, a, roll(b, 4, 0))
                    y = jnp.where(low_half, roll(a, 4, 0), b)
                    q_ref[p, k, j, 2 * h] = x
                    q_ref[p, k, j, 2 * h + 1] = y
                    tops.append(jnp.maximum(x, y))
                    bottoms.append(jnp.minimum(x, y))
        while len(tops) > 1:
            tops = [jnp.maximum(x, y) for x, y in zip(tops[::2], tops[1::2])]
            bottoms = [jnp.minimum(x, y) for x, y in zip(bottoms[::2], bottoms[1::2])]
        ext_ref[0, p] = tops[0]
        ext_ref[1, p] = bottoms[0]
        for axis in AXES:
            put(
                messages,
                axis,
                EXT + p,
                pack_high(tops[0], bottoms[0], STEP[axis]),
                pack_low(tops[0], bottoms[0], STEP[axis]),
            )
        put_faces(q_ref, p, messages, 0)
        tendency(q_ref, s_ref, p, coef, no_halo, no_halo, finish)
        put_faces(s_ref, p, messages, FACE)
        return carry

    lax.fori_loop(0, 3, pair, 0)


def bounds(ext_ref, messages, p):
    top, bottom = ext_ref[0, p], ext_ref[1, p]
    upper = jnp.maximum(top, jnp.maximum(roll(top, 1, 1), roll(top, -1, 1)))
    lower = jnp.minimum(bottom, jnp.minimum(roll(bottom, 1, 1), roll(bottom, -1, 1)))
    for axis in AXES:
        dn, up = beside(top, top, *get_single(messages, axis, EXT + p, 0), STEP[axis])
        upper = jnp.maximum(upper, jnp.maximum(dn, up))
        dn, up = beside(bottom, bottom, *get_single(messages, axis, EXT + p, 1), STEP[axis])
        lower = jnp.minimum(lower, jnp.minimum(dn, up))
    return upper, lower


def outer(pair, step):
    return jnp.where(bit(pair[0].shape, step), pair[1], pair[0])


def first_kernel(q_ref, part_ref, speeds_ref, ext_ref, *refs):
    got, (out_ref, limit_ref, corner_ref, weight_ref) = refs[:4], refs[4:8]
    messages, s_ref = refs[8:12], refs[12]
    coef = coefficients(speeds_ref)
    in_y, to_y = rim_coefficients(coef[1], 1)
    in_z, to_z = rim_coefficients(coef[2], 2)
    in_zn, to_zn = [outer(get_single(got, "dev", COEF, h), 1) for h in range(2)]
    in_ym, to_ym = [outer(get_single(got, "grp", COEF, h), 2) for h in range(2)]
    weight_ref[...] = 0.25 * (in_y * in_zn + in_z * in_ym)
    weight_n = 0.25 * (to_y * in_z + in_zn * to_ym)
    weight_m = 0.25 * (to_z * in_y + in_ym * to_zn)
    high_y, high_z = bit((8, 128), 1), bit((8, 128), 2)
    y_in = [jnp.where(high_y, 0.0, in_y), jnp.where(high_y, in_y, 0.0)]
    z_in = [jnp.where(high_z, 0.0, in_z), jnp.where(high_z, in_z, 0.0)]

    def halo_y(p, k):
        dn, up = get_face(got, "dev", p, k, FACE)
        return dn + to_y * q_ref[p, k, 0], up + to_y * q_ref[p, k, 3]

    def halo_z(p, j):
        dn, up = get_face(got, "grp", p, j, FACE)
        return dn + to_z * q_ref[p, 0, j], up + to_z * q_ref[p, 3, j]

    def finish(p, k, j, s, t):
        out_ref[p, k, j] = 0.75 * q_ref[p, k, j] + 0.25 * (s + t)

    def pair(p, carry):
        edges_y, edges_z = {}, {}
        for k in range(4):
            dn, up = get_face(got, "dev", p, k, 0)
            s_ref[p, k, 0] = part_ref[p, k, 0] + y_in[0] * dn
            s_ref[p, k, 1] = part_ref[p, k, 1]
            s_ref[p, k, 2] = part_ref[p, k, 2]
            s_ref[p, k, 3] = part_ref[p, k, 3] + y_in[1] * up
            if k in (0, 3):
                edges_y[k] = outer((dn, up), 1)
        for j in range(4):
            dn, up = get_face(got, "grp", p, j, 0)
            s_ref[p, 0, j] = s_ref[p, 0, j] + z_in[0] * dn
            s_ref[p, 3, j] = s_ref[p, 3, j] + z_in[1] * up
            if j in (0, 3):
                edges_z[j] = outer((dn, up), 2)
        edge_n = jnp.where(high_z, edges_y[3], edges_y[0])
        edge_m = jnp.where(high_y, edges_z[3], edges_z[0])
        corner_ref[0, p] = weight_n * edge_m
        corner_ref[1, p] = weight_m * edge_n
        put(
            messages,
            "dev",
            pl.ds(FACE + 2 * p, 2),
            pack_high(edge_m[:2], edge_m[2:], 1),
            pack_low(edge_m[:2], edge_m[2:], 1),
        )
        tendency(s_ref, out_ref, p, coef, halo_y, halo_z, finish)
        put_faces(out_ref, p, messages, 0)
        upper, lower = bounds(ext_ref, got, p)
        limit_ref[0, p] = upper
        limit_ref[1, p] = lower
        return carry

    lax.fori_loop(0, 3, pair, 0)


def operator_kernel(sharpen_ref, high_ref, low_ref):
    s = sharpen_ref[...]
    high = s.astype(jnp.bfloat16)
    low = (s - high.astype(jnp.float32)).astype(jnp.bfloat16)
    rows = lax.broadcasted_iota(jnp.int32, (256, 64), 0)
    cols = lax.broadcasted_iota(jnp.int32, (256, 64), 1)
    tall = (rows // 4 == cols).astype(jnp.bfloat16)
    rows = lax.broadcasted_iota(jnp.int32, (64, 256), 0)
    cols = lax.broadcasted_iota(jnp.int32, (64, 256), 1)
    wide = (cols // 4 == rows).astype(jnp.bfloat16)
    rows = lax.broadcasted_iota(jnp.int32, (256, 256), 0)
    cols = lax.broadcasted_iota(jnp.int32, (256, 256), 1)
    same = (rows & 3) == (cols & 3)
    for part, ref in ((high, high_ref), (low, low_ref)):
        half = jnp.dot(tall, part, preferred_element_type=jnp.float32).astype(jnp.bfloat16)
        full = jnp.dot(half, wide, preferred_element_type=jnp.float32)
        ref[...] = jnp.where(same, full, 0.0).astype(jnp.bfloat16)


def last_kernel(
    q_ref, part_ref, speeds_ref, limit_ref, corner_ref, weight_ref, count_ref, high_ref, low_ref, *refs
):
    got, out_hbm, (s_ref, acc_ref, off_ref, out_ref, sems) = refs[:4], refs[4], refs[5:]

    def part(p):
        at = pl.ds(2 * p, 2)
        return pltpu.make_async_copy(out_ref.at[at], out_hbm.at[at], sems.at[p])

    coef = coefficients(speeds_ref)
    low_half = sublane((8, 128)) < 4
    high_y, high_z = bit((8, 128), 1), bit((8, 128), 2)
    at_y = {0: jnp.logical_not(high_y), 3: high_y}
    at_z = {0: jnp.logical_not(high_z), 3: high_z}

    def halo_y(p, k):
        dn, up = get_face(got, "dev", p, k, 0)
        if k in at_z:
            more = jnp.where(at_z[k], corner_ref[0, p], 0.0)
            dn, up = dn + more, up + more
        return dn, up

    def halo_z(p, j):
        dn, up = get_face(got, "grp", p, j, 0)
        if j in at_y:
            more = jnp.where(at_y[j], corner_ref[1, p], 0.0)
            dn, up = dn + more, up + more
        return dn, up

    def finish(p, k, j, s, t):
        acc_ref[p, k, j] = q_ref[p, k, j] * (1.0 / 3.0) + (2.0 / 3.0) * (s + t)

    def pair(p, carry):
        at = pl.ds(FACE + 2 * p, 2)
        edge = jnp.concatenate(
            [outer(get_single(got, "dev", at, h), 1) for h in range(2)], axis=0
        )
        edge = weight_ref[...] * edge
        for k in range(4):
            for j in range(4):
                value = part_ref[p, k, j]
                if k in at_z and j in at_y:
                    value = value + jnp.where(jnp.logical_and(at_z[k], at_y[j]), edge, 0.0)
                s_ref[p, k, j] = value
        tendency(s_ref, acc_ref, p, coef, halo_y, halo_z, finish)
        return carry

    lax.fori_loop(0, 3, pair, 0)

    counts = count_ref[...]
    present = [(counts > float(f)).astype(jnp.float32) for f in range(6)]
    share = 1.0 / counts

    def node_pair(k, carry):
        for j in range(4):
            for h in range(2):
                m = 8 * k + 2 * j + h
                rows = []
                for p in range(3):
                    x = acc_ref[p, k, j, 2 * h]
                    y = acc_ref[p, k, j, 2 * h + 1]
                    rows.append(jnp.where(low_half, x, roll(y, 4, 0)))
                    rows.append(jnp.where(low_half, roll(x, 4, 0), y))
                mean = rows[0] * present[0]
                for f in range(1, 6):
                    mean = mean + rows[f] * present[f]
                mean = mean * share
                for f in range(6):
                    out_ref[f, m] = rows[f]
                    off_ref[f, m] = (rows[f] - mean) * present[f]
        return carry

    lax.fori_loop(0, 4, node_pair, 0)

    high, low = high_ref[...], low_ref[...]
    for p in range(3):
        off = jnp.concatenate(
            [off_ref[2 * p].reshape(256, 128), off_ref[2 * p + 1].reshape(256, 128)], axis=1
        )
        off_high = off.astype(jnp.bfloat16)
        off_low = (off - off_high.astype(jnp.float32)).astype(jnp.bfloat16)
        fix = jnp.dot(high, off_high, preferred_element_type=jnp.float32)
        fix = fix + jnp.dot(high, off_low, preferred_element_type=jnp.float32)
        fix = fix + jnp.dot(low, off_high, preferred_element_type=jnp.float32)
        upper, lower = limit_ref[0, p], limit_ref[1, p]
        for h in range(2):
            u, v = roll(upper, 4, 0), roll(lower, 4, 0)
            if h == 0:
                u, v = jnp.where(low_half, upper, u), jnp.where(low_half, lower, v)
            else:
                u, v = jnp.where(low_half, u, upper), jnp.where(low_half, v, lower)
            f = 2 * p + h
            value = out_ref[f] + fix[:, 128 * h : 128 * h + 128].reshape(32, 8, 128)
            out_ref[f] = jnp.minimum(jnp.maximum(value, v), u)
        part(p).start()
    for p in range(3):
        part(p).wait()


def call(kernel, outs, args, scratch=(), flops=5_000_000, space=pltpu.VMEM, out_space=pltpu.VMEM):
    return pl.pallas_call(
        kernel,
        out_shape=[jax.ShapeDtypeStruct(*o) for o in outs],
        in_specs=[pl.BlockSpec(memory_space=space)] * len(args),
        out_specs=[pl.BlockSpec(memory_space=out_space)] * len(outs),
        scratch_shapes=[pltpu.VMEM(*s) if isinstance(s, tuple) else s for s in scratch],
        compiler_params=pltpu.CompilerParams(vmem_limit_bytes=LIMIT),
        cost_estimate=pl.CostEstimate(flops=flops, bytes_accessed=2_000_000, transcendentals=0),
    )(*args)


EVEN_PAIRS = [(i, i ^ 1) for i in range(16)]
ODD_PAIRS = [((i + 1) % 16, ((i ^ 1) + 1) % 16) for i in range(16)]


def exchange(messages):
    ways = (("dev", ODD_PAIRS), ("dev", EVEN_PAIRS), ("grp", ODD_PAIRS), ("grp", EVEN_PAIRS))
    return [lax.ppermute(m, axis, pairs) for m, (axis, pairs) in zip(messages, ways)]


def shards(fields, speeds, sharpen, mat_count):
    f32, bf16 = jnp.float32, jnp.bfloat16
    rows = fields.reshape(ROW)
    speeds = speeds.reshape(24, 128)
    counts = mat_count.reshape(4, 128)
    node, one, ext = (NODE, f32), ((8, 128), f32), ((2, 3, 8, 128), f32)
    corner = ((2, 3, 4, 8, 128), f32)
    high, low = call(operator_kernel, [((256, 256), bf16)] * 2, [sharpen])
    arguments = [pltpu.with_memory_space_constraint(x, pltpu.HBM) for x in (rows, speeds, counts)]
    q, s, extremes, counts, speeds, *messages = call(
        open_kernel,
        [node, node, ext, one, ((24, 128), f32)] + [((COEF + 1, 8, 128), f32)] * 4,
        arguments,
        scratch=[(ROW, f32), ((4, 128), jnp.int32), pltpu.SemaphoreType.DMA((5,))],
        space=pltpu.HBM,
    )
    got = exchange(messages)
    s, limits, corners, weight, *messages = call(
        first_kernel,
        [node, ext, corner, one] + [((FACE + 6, 8, 128), f32)] * 2 + [((FACE, 8, 128), f32)] * 2,
        [q, s, speeds, extremes, *got],
        scratch=[node],
    )
    got = exchange(messages)
    (out,) = call(
        last_kernel,
        [(ROW, f32)],
        [q, s, speeds, limits, corners, weight, counts, high, low, *got],
        scratch=[node, node, (ROW, f32), (ROW, f32), pltpu.SemaphoreType.DMA((3,))],
        out_space=pltpu.HBM,
    )
    return out.reshape(fields.shape)


def solution(mesh):
    in_specs = (
        P(None, None, "grp", "dev", None),
        P(None, None, "grp", "dev", None),
        P(),
        P("grp", "dev", None),
    )
    out_specs = P(None, None, "grp", "dev", None)
    return jax.shard_map(shards, mesh=mesh, in_specs=in_specs, out_specs=out_specs, check_vma=False)
```

```python
import functools

import jax
import jax.numpy as jnp
import numpy as np
from jax import lax
from jax.experimental import pallas as pl
from jax.experimental.pallas import tpu as pltpu
from jax.sharding import PartitionSpec as P

DT = 0.08
LIFT = 6.0
NODE = (3, 4, 4, 4, 8, 128)
ROW = (6, 32, 8, 128)
FACE = 24
EXT = 2 * FACE
COEF = EXT + 3
STEP = {"dev": 1, "grp": 2}
LIMIT = 48 * 1024 * 1024


def gll_derivative():
    points = np.array([-1.0, -1.0 / np.sqrt(5.0), 1.0 / np.sqrt(5.0), 1.0])
    products = np.array(
        [
            np.prod([points[first] - points[second] for second in range(4) if second != first])
            for first in range(4)
        ]
    )
    matrix = np.zeros((4, 4))
    for first in range(4):
        for second in range(4):
            if first != second:
                matrix[first, second] = (
                    products[first] / products[second] / (points[first] - points[second])
                )
        matrix[first, first] = sum(
            (1.0 / (points[first] - points[other]) for other in range(4) if other != first)
        )
    return matrix


D = gll_derivative()
SCALE = [float(x) / 2 for x in (D[0, 0] + D[0, 3], D[0, 0] - D[0, 3], D[0, 1] - D[0, 2])]
RATIO = [float(x) / 2 / s for x, s in zip((D[1, 0] + D[1, 3], D[1, 0] - D[1, 3], D[1, 1] - D[1, 2]), SCALE)]


def roll(x, shift, axis):
    size = x.shape[axis]
    return pltpu.roll(x, shift % size, axis)


def sublane(shape):
    return lax.broadcasted_iota(jnp.int32, shape, len(shape) - 2)


def bit(shape, step):
    return (sublane(shape) & step) != 0


def even_device(axis):
    return lax.rem(lax.axis_index(axis), 2) == 0


def coefficients(speeds_ref, factor=1.0):
    out = []
    low_half = sublane((8, 128)) < 4
    for d in range(3):
        v = speeds_ref[pl.ds(8 * d, 8), :]
        w = roll(v, 4, 0)
        a = jnp.where(low_half, v, w)
        b = jnp.where(low_half, w, v)
        c = 0.5 * (a + b)
        dt = DT * factor
        out.append(
            (
                -dt * c,
                (-dt * LIFT) * (c - jnp.minimum(a, 0.0)),
                (dt * LIFT) * jnp.maximum(a, 0.0),
                (-dt * LIFT) * (jnp.maximum(b, 0.0) - c),
                (-dt * LIFT) * jnp.minimum(b, 0.0),
                (-dt * LIFT) * jnp.minimum(a, 0.0),
                (dt * LIFT) * jnp.maximum(b, 0.0),
            )
        )
    return out


def rim_coefficients(coef, step):
    upper = bit((8, 128), step)
    return jnp.where(upper, coef[4], coef[2]), jnp.where(upper, coef[6], coef[5])


def local(coef, step):
    c, low, low_in, high, high_in = coef[:5]
    if step:
        upper = bit((8, 128), step)
        low_in, high_in = jnp.where(upper, low_in, 0.0), jnp.where(upper, 0.0, high_in)
    return [c * s for s in SCALE], low, low_in, high, high_in, step


def line(q, c):
    t = c[0] * ((q[0] + q[3]) - (q[1] + q[2]))
    o0 = c[1] * (q[0] - q[3])
    o1 = c[2] * (q[1] - q[2])
    e = RATIO[0] * t
    o = RATIO[1] * o0 + RATIO[2] * o1
    o0 = o0 + o1
    return [o0 + t, o + e, o - e, o0 - t]


def with_faces(q, coef):
    c, low, low_in, high, high_in, step = coef
    axis = q[0].ndim - 2 if step else q[0].ndim - 1
    step = step if step else 1
    r = line(q, c)
    r[0] = r[0] + (low * q[0] + low_in * roll(q[3], step, axis))
    r[3] = r[3] + (high * q[3] + high_in * roll(q[0], -step, axis))
    return r


def beside(low, high, halo_dn, halo_up, step):
    upper = bit(low.shape, step)
    dn = jnp.where(upper, roll(high, step, low.ndim - 2), halo_dn)
    up = jnp.where(upper, halo_up, roll(low, -step, low.ndim - 2))
    return dn, up


def pack_high(a, b, step):
    return jnp.where(bit(a.shape, step), b, roll(a, -step, a.ndim - 2))


def pack_low(a, b, step):
    return jnp.where(bit(a.shape, step), roll(a, step, a.ndim - 2), b)


def unpack_dn(m, second, step):
    return roll(m, -step, m.ndim - 2) if second else m


def unpack_up(m, second, step):
    return roll(m, step, m.ndim - 2) if second else m


def tendency(q_ref, acc_ref, p, coef, finish):
    along_x, along_y, along_z = [local(coef[d], d) for d in range(3)]
    for k in range(4):
        rx = with_faces([q_ref[p, k, :, i] for i in range(4)], along_x)
        for i in range(4):
            acc_ref[p, k, :, i] = rx[i]
        ry = with_faces([q_ref[p, k, j] for j in range(4)], along_y)
        for j in range(4):
            acc_ref[p, k, j] = acc_ref[p, k, j] + ry[j]
    for j in range(4):
        qz = [q_ref[p, k, j] for k in range(4)]
        rz = with_faces(qz, along_z)
        for k in range(4):
            finish(p, k, j, qz[k], acc_ref[p, k, j] + rz[k])


AXES = ("dev", "grp")
WAYS = (("dev", 1), ("dev", 0), ("grp", 1), ("grp", 0))


def put(messages, axis, at, to_next, to_last):
    even = even_device(axis)
    first, second = [messages[WAYS.index((axis, odd))] for odd in (0, 1)]
    first[at] = jnp.where(even, to_next, to_last)
    second[at] = jnp.where(even, to_last, to_next)


def get(messages, axis, at):
    even = even_device(axis)
    first, second = [messages[WAYS.index((axis, odd))] for odd in (0, 1)]
    x, y = first[at], second[at]
    return jnp.where(even, y, x), jnp.where(even, x, y)


def get_single(messages, axis, at, second):
    last, after = get(messages, axis, at)
    step = STEP[axis]
    return unpack_dn(last, second, step), unpack_up(after, second, step)


def face(q_ref, p, axis, side, plane):
    return q_ref[p, plane, side] if axis == "dev" else q_ref[p, side, plane]


def put_faces(q_ref, p, messages, base):
    for axis in AXES:
        step = STEP[axis]
        for half in range(2):
            m = 2 * half
            low = [face(q_ref, p, axis, 0, m + h) for h in range(2)]
            high = [face(q_ref, p, axis, 3, m + h) for h in range(2)]
            put(
                messages,
                axis,
                pl.ds(base + 8 * p + 4 * half, 4),
                pack_high(high[0], high[1], step),
                pack_low(low[0], low[1], step),
            )


def get_face(messages, axis, p, plane, base):
    at = pl.ds(base + 8 * p + 4 * (plane // 2), 4)
    return get_single(messages, axis, at, plane % 2)


def open_kernel(fields_hbm, speeds_hbm, count_hbm, *refs):
    q_ref, s_ref, ext_ref, wide_count_ref, speeds_ref = refs[:5]
    messages, (fields_ref, count_ref, sems) = refs[5:9], refs[9:]
    copies = [
        pltpu.make_async_copy(speeds_hbm, speeds_ref, sems.at[3]),
        pltpu.make_async_copy(count_hbm, count_ref, sems.at[4]),
    ]

    def part(p):
        at = pl.ds(2 * p, 2)
        return pltpu.make_async_copy(fields_hbm.at[at], fields_ref.at[at], sems.at[p])

    for copy in copies + [part(p) for p in range(3)]:
        copy.start()
    for copy in copies:
        copy.wait()
    low_half = sublane((8, 128)) < 4
    coef = coefficients(speeds_ref)
    counts = count_ref[...].astype(jnp.float32)
    wide_count_ref[...] = jnp.concatenate([counts, counts], axis=0)
    for axis, d in (("dev", 2), ("grp", 1)):
        pair = rim_coefficients(coef[d], STEP[AXES[d - 1]])
        put(
            messages,
            axis,
            COEF,
            pack_high(pair[0], pair[1], STEP[axis]),
            pack_low(pair[0], pair[1], STEP[axis]),
        )

    def finish(p, k, j, q, t):
        s_ref[p, k, j] = q + t

    def pair(p, carry):
        part(p).wait()
        tops, bottoms = [], []
        for k in range(4):
            for j in range(4):
                for h in range(2):
                    m = 8 * k + 2 * j + h
                    a = fields_ref[2 * p, m]
                    b = fields_ref[2 * p + 1, m]
                    x = jnp.where(low_half, a, roll(b, 4, 0))
                    y = jnp.where(low_half, roll(a, 4, 0), b)
                    q_ref[p, k, j, 2 * h] = x
                    q_ref[p, k, j, 2 * h + 1] = y
                    tops.append(jnp.maximum(x, y))
                    bottoms.append(jnp.minimum(x, y))
        while len(tops) > 1:
            tops = [jnp.maximum(x, y) for x, y in zip(tops[::2], tops[1::2])]
            bottoms = [jnp.minimum(x, y) for x, y in zip(bottoms[::2], bottoms[1::2])]
        ext_ref[0, p] = tops[0]
        ext_ref[1, p] = bottoms[0]
        for axis in AXES:
            put(
                messages,
                axis,
                EXT + p,
                pack_high(tops[0], bottoms[0], STEP[axis]),
                pack_low(tops[0], bottoms[0], STEP[axis]),
            )
        put_faces(q_ref, p, messages, 0)
        tendency(q_ref, s_ref, p, coef, finish)
        put_faces(s_ref, p, messages, FACE)
        return carry

    lax.fori_loop(0, 3, pair, 0)


def bounds(ext_ref, messages, p):
    top, bottom = ext_ref[0, p], ext_ref[1, p]
    upper = jnp.maximum(top, jnp.maximum(roll(top, 1, 1), roll(top, -1, 1)))
    lower = jnp.minimum(bottom, jnp.minimum(roll(bottom, 1, 1), roll(bottom, -1, 1)))
    for axis in AXES:
        dn, up = beside(top, top, *get_single(messages, axis, EXT + p, 0), STEP[axis])
        upper = jnp.maximum(upper, jnp.maximum(dn, up))
        dn, up = beside(bottom, bottom, *get_single(messages, axis, EXT + p, 1), STEP[axis])
        lower = jnp.minimum(lower, jnp.minimum(dn, up))
    return upper, lower


def outer(pair, step):
    return jnp.where(bit(pair[0].shape, step), pair[1], pair[0])


def spread(coef, step):
    upper = bit((8, 128), step)
    c, low, _, high = coef[:4]
    out = [c * jnp.where(upper, float(D[n, 3]), float(D[n, 0])) for n in range(4)]
    out[0] = out[0] + jnp.where(upper, 0.0, low)
    out[3] = out[3] + jnp.where(upper, high, 0.0)
    return out


def along_plane(h, along_x, along_t):
    out = with_faces(h, along_t)
    for t in range(4):
        out[t] = out[t] + jnp.stack(with_faces([h[t][i] for i in range(4)], along_x))
    return out


def local_kernel(q_ref, part_ref, speeds_ref, sharpen_ref, out_ref, *operators):
    coef = coefficients(speeds_ref, 0.25)
    build_operators(sharpen_ref, *operators)

    def finish(p, k, j, s, t):
        out_ref[p, k, j] = (0.75 * q_ref[p, k, j] + 0.25 * s) + t

    def pair(p, carry):
        tendency(part_ref, out_ref, p, coef, finish)
        return carry

    lax.fori_loop(0, 3, pair, 0)


def first_kernel(q_ref, base_ref, speeds_ref, *refs):
    got, (out_ref, corner_ref, weight_ref), messages = refs[:4], refs[4:7], refs[7:]
    coef = coefficients(speeds_ref)
    in_y, to_y = rim_coefficients(coef[1], 1)
    in_z, to_z = rim_coefficients(coef[2], 2)
    in_zn, to_zn = [outer(get_single(got, "dev", COEF, h), 1) for h in range(2)]
    in_ym, to_ym = [outer(get_single(got, "grp", COEF, h), 2) for h in range(2)]
    weight_ref[...] = 0.25 * (in_y * in_zn + in_z * in_ym)
    weight_n = 0.25 * (to_y * in_z + in_zn * to_ym)
    weight_m = 0.25 * (to_z * in_y + in_ym * to_zn)
    high_y, high_z = bit((8, 128), 1), bit((8, 128), 2)
    some_y, some_z = 0.25 * in_y, 0.25 * in_z
    along = [local(coef[d], d) for d in range(3)]
    spread_y, spread_z = spread(coef[1], 1), spread(coef[2], 2)

    def pair(p, carry):
        from_n = [outer(get_face(got, "dev", p, k, 0), 1) for k in range(4)]
        from_m = [outer(get_face(got, "grp", p, j, 0), 2) for j in range(4)]
        edge_n = jnp.where(high_z, from_n[3], from_n[0])
        edge_m = jnp.where(high_y, from_m[3], from_m[0])
        corner_ref[0, p] = weight_n * edge_m
        corner_ref[1, p] = weight_m * edge_n
        put(
            messages,
            "dev",
            pl.ds(FACE + 2 * p, 2),
            pack_high(edge_m[:2], edge_m[2:], 1),
            pack_low(edge_m[:2], edge_m[2:], 1),
        )
        hy = [some_y * x for x in from_n]
        hz = [some_z * x for x in from_m]
        plane_y = along_plane(hy, along[0], along[2])
        plane_z = along_plane(hz, along[0], along[1])
        for n in range(4):
            own = jnp.where(high_y, q_ref[p, n, 3], q_ref[p, n, 0])
            ghost = outer(get_face(got, "dev", p, n, FACE), 1) + to_y * own
            plane_y[n] = plane_y[n] + (hy[n] + some_y * ghost)
            own = jnp.where(high_z, q_ref[p, 3, n], q_ref[p, 0, n])
            ghost = outer(get_face(got, "grp", p, n, FACE), 2) + to_z * own
            plane_z[n] = plane_z[n] + (hz[n] + some_z * ghost)
        for k in range(4):
            for j in range(4):
                value = base_ref[p, k, j] + (spread_y[j] * hy[k] + spread_z[k] * hz[j])
                if j in (0, 3):
                    value = value + jnp.where(high_y == (j == 3), plane_y[k], 0.0)
                if k in (0, 3):
                    value = value + jnp.where(high_z == (k == 3), plane_z[j], 0.0)
                out_ref[p, k, j] = value
        put_faces(out_ref, p, messages, 0)
        return carry

    lax.fori_loop(0, 3, pair, 0)


def build_operators(sharpen_ref, high_ref, low_ref, rim_ref, rim_low_ref):
    f32, bf16 = jnp.float32, jnp.bfloat16

    def index(shape, axis):
        return lax.broadcasted_iota(jnp.int32, shape, axis)

    tall = (index((256, 64), 0) // 4 == index((256, 64), 1)).astype(bf16)
    wide = (index((64, 256), 1) // 4 == index((64, 256), 0)).astype(f32)
    node, col = index((64, 128), 0), index((64, 128), 1)
    t, i = (col >> 4) & 3, (col >> 2) & 3
    on_y = 16 * t + 12 * (col & 1) + i
    on_z = 48 * ((col >> 1) & 1) + 4 * t + i
    pick = (node == jnp.where(col < 64, on_y, on_z)).astype(f32)
    wide = jnp.concatenate([wide, pick], axis=1).astype(bf16)
    same = (index((256, 128), 0) & 3) == (index((256, 128), 1) & 3)
    for part, ref in zip(split(sharpen_ref[...]), (high_ref, low_ref)):
        half = jnp.dot(tall, part, preferred_element_type=f32).astype(bf16)
        full = jnp.dot(half, wide, preferred_element_type=f32)
        full = [jnp.where(same, full[:, 128 * n : 128 * n + 128], 0.0).astype(bf16) for n in range(3)]
        ref[...] = jnp.concatenate(full[:2], axis=1)
        if ref is high_ref:
            rim_ref[...] = jnp.concatenate([full[2], full[2]], axis=1)
        else:
            rim_low_ref[...] = full[2]


def split(x):
    high = x.astype(jnp.bfloat16)
    return high, (x - high.astype(jnp.float32)).astype(jnp.bfloat16)


def to_rows(pairs):
    low_half = sublane((8, 128)) < 4
    rows = []
    for x, y in pairs:
        rows.append(jnp.where(low_half, x, roll(y, 4, 0)))
        rows.append(jnp.where(low_half, roll(x, 4, 0), y))
    return rows


def presence(count_ref):
    counts = count_ref[...]
    return [(counts > float(f)).astype(jnp.float32) for f in range(6)], 1.0 / counts


def offsets(rows, present, share):
    mean = rows[0] * present[0]
    for f in range(1, 6):
        mean = mean + rows[f] * present[f]
    mean = mean * share
    return [(rows[f] - mean) * present[f] for f in range(6)]


def columns(ref, p, rows):
    return jnp.concatenate([ref[2 * p].reshape(rows, 128), ref[2 * p + 1].reshape(rows, 128)], axis=1)


def inner_kernel(q_ref, part_ref, speeds_ref, ext_ref, count_ref, high_ref, low_ref, *refs):
    got, (out_ref, limit_ref, acc_ref, off_ref) = refs[:4], refs[4:]
    coef = coefficients(speeds_ref, 2.0 / 3.0)
    low_half = sublane((8, 128)) < 4

    def finish(p, k, j, s, t):
        acc_ref[p, k, j] = (q_ref[p, k, j] * (1.0 / 3.0) + (2.0 / 3.0) * s) + t

    def pair(p, carry):
        tendency(part_ref, acc_ref, p, coef, finish)
        for n, x in enumerate(bounds(ext_ref, got, p)):
            y = roll(x, 4, 0)
            limit_ref[n, 2 * p] = jnp.where(low_half, x, y)
            limit_ref[n, 2 * p + 1] = jnp.where(low_half, y, x)
        return carry

    lax.fori_loop(0, 3, pair, 0)
    present, share = presence(count_ref)

    def node_pair(k, carry):
        for j in range(4):
            for h in range(2):
                m = 8 * k + 2 * j + h
                rows = to_rows([(acc_ref[p, k, j, 2 * h], acc_ref[p, k, j, 2 * h + 1]) for p in range(3)])
                off = offsets(rows, present, share)
                for f in range(6):
                    out_ref[f, m] = rows[f]
                    off_ref[f, m] = off[f]
        return carry

    lax.fori_loop(0, 4, node_pair, 0)
    high, low = high_ref[...], low_ref[...]
    for p in range(3):
        off_high, off_low = split(columns(off_ref, p, 256))
        fix = jnp.dot(high, off_high, preferred_element_type=jnp.float32)
        fix = fix + jnp.dot(high, off_low, preferred_element_type=jnp.float32)
        fix = fix + jnp.dot(low, off_high, preferred_element_type=jnp.float32)
        for h in range(2):
            f = 2 * p + h
            out_ref[f] = out_ref[f] + fix[:, 128 * h : 128 * h + 128].reshape(32, 8, 128)


def last_kernel(
    base_ref, speeds_ref, limit_ref, corner_ref, weight_ref, count_ref, rim_ref, rim_low_ref, *refs
):
    got, out_hbm, (plane_ref, off_ref, out_ref, sems) = refs[:4], refs[4], refs[5:]

    def part(p):
        at = pl.ds(2 * p, 2)
        return pltpu.make_async_copy(out_ref.at[at], out_hbm.at[at], sems.at[p])

    coef = coefficients(speeds_ref)
    in_y, _ = rim_coefficients(coef[1], 1)
    in_z, _ = rim_coefficients(coef[2], 2)
    high_y, high_z = bit((8, 128), 1), bit((8, 128), 2)
    some_y, some_z = (2.0 / 3.0) * in_y, (2.0 / 3.0) * in_z
    spread_y, spread_z = spread(coef[1], 1), spread(coef[2], 2)
    weight = (2.0 / 3.0) * weight_ref[...]
    present, share = presence(count_ref)

    planes = []
    for p in range(3):
        at = pl.ds(FACE + 2 * p, 2)
        late = weight * jnp.concatenate(
            [outer(get_single(got, "dev", at, h), 1) for h in range(2)], axis=0
        )
        x = with_faces([late[i] for i in range(4)], local(coef[0], 0))
        at_corner = late + jnp.stack(x) + some_y * corner_ref[0, p]
        to_corner = some_z * corner_ref[1, p]
        both = []
        for k in range(4):
            value = some_y * outer(get_face(got, "dev", p, k, 0), 1) + spread_z[k] * late
            if k in (0, 3):
                value = value + jnp.where(high_z == (k == 3), at_corner, 0.0)
            both.append(value)
        for j in range(4):
            value = some_z * outer(get_face(got, "grp", p, j, 0), 2) + spread_y[j] * late
            if j in (0, 3):
                value = value + jnp.where(high_y == (j == 3), to_corner, 0.0)
            both.append(value)
        planes.append(both)
    for t in range(8):
        for h in range(2):
            rows = to_rows([(planes[p][t][2 * h], planes[p][t][2 * h + 1]) for p in range(3)])
            off = offsets(rows, present, share)
            for f in range(6):
                plane_ref[f, 2 * t + h] = rows[f]
                off_ref[f, 2 * t + h] = off[f]

    rim, rim_low = rim_ref[...], rim_low_ref[...]
    for p in range(3):
        off_high, off_low = split(columns(off_ref, p, 128))
        fix = jnp.dot(rim, jnp.concatenate([off_high, off_low], axis=0), preferred_element_type=jnp.float32)
        fix = fix + jnp.dot(rim_low, off_high, preferred_element_type=jnp.float32)
        for g in range(2):
            f = 2 * p + g
            part_fix = fix[:, 128 * g : 128 * g + 128].reshape(4, 4, 2, 8, 128)
            for k in range(4):
                for j in range(4):
                    at = pl.ds(8 * k + 2 * j, 2)
                    value = base_ref[f, at] + part_fix[k, j]
                    if j in (0, 3):
                        value = value + jnp.where(high_y == (j == 3), plane_ref[f, pl.ds(2 * k, 2)], 0.0)
                    if k in (0, 3):
                        value = value + jnp.where(
                            high_z == (k == 3), plane_ref[f, pl.ds(8 + 2 * j, 2)], 0.0
                        )
                    out_ref[f, at] = jnp.minimum(jnp.maximum(value, limit_ref[1, f]), limit_ref[0, f])
        part(p).start()
    for p in range(3):
        part(p).wait()


def call(kernel, outs, args, scratch=(), flops=5_000_000, space=pltpu.VMEM, out_space=pltpu.VMEM):
    return pl.pallas_call(
        kernel,
        out_shape=[jax.ShapeDtypeStruct(*o) for o in outs],
        in_specs=[pl.BlockSpec(memory_space=space)] * len(args),
        out_specs=[pl.BlockSpec(memory_space=out_space)] * len(outs),
        scratch_shapes=[pltpu.VMEM(*s) if isinstance(s, tuple) else s for s in scratch],
        compiler_params=pltpu.CompilerParams(vmem_limit_bytes=LIMIT),
        cost_estimate=pl.CostEstimate(flops=flops, bytes_accessed=2_000_000, transcendentals=0),
    )(*args)


EVEN_PAIRS = [(i, i ^ 1) for i in range(16)]
ODD_PAIRS = [((i + 1) % 16, ((i ^ 1) + 1) % 16) for i in range(16)]


def exchange(messages):
    pairs = (EVEN_PAIRS, ODD_PAIRS)
    return [lax.ppermute(m, axis, pairs[odd]) for m, (axis, odd) in zip(messages, WAYS)]


def shards(fields, speeds, sharpen, mat_count):
    f32, bf16 = jnp.float32, jnp.bfloat16
    rows = fields.reshape(ROW)
    speeds = speeds.reshape(24, 128)
    counts = mat_count.reshape(4, 128)
    node, one, ext = (NODE, f32), ((8, 128), f32), ((2, 3, 8, 128), f32)
    corner = ((2, 3, 4, 8, 128), f32)
    q, s, extremes, counts, speeds, *messages = call(
        open_kernel,
        [node, node, ext, one, ((24, 128), f32)] + [((COEF + 1, 8, 128), f32)] * 4,
        [pltpu.with_memory_space_constraint(x, pltpu.HBM) for x in (rows, speeds, counts)],
        scratch=[(ROW, f32), ((4, 128), jnp.int32), pltpu.SemaphoreType.DMA((5,))],
        space=pltpu.HBM,
    )
    first = exchange(messages)
    square = ((256, 256), bf16)
    base, high, low, rim, rim_low = call(
        local_kernel, [node, square, square, square, ((256, 128), bf16)], [q, s, speeds, sharpen]
    )
    s, corners, weight, *messages = call(
        first_kernel,
        [node, corner, one] + [((FACE + (6 if axis == "dev" else 0), 8, 128), f32) for axis, _ in WAYS],
        [q, base, speeds, *first],
    )
    second = exchange(messages)
    base, limits = call(
        inner_kernel,
        [(ROW, f32), ((2, 6, 8, 128), f32)],
        [q, s, speeds, extremes, counts, high, low, *first],
        scratch=[node, (ROW, f32)],
    )
    plane = ((6, 16, 8, 128), f32)
    (out,) = call(
        last_kernel,
        [(ROW, f32)],
        [base, speeds, limits, corners, weight, counts, rim, rim_low, *second],
        scratch=[plane, plane, (ROW, f32), pltpu.SemaphoreType.DMA((3,))],
        out_space=pltpu.HBM,
    )
    return out.reshape(fields.shape)


def solution(mesh):
    in_specs = (
        P(None, None, "grp", "dev", None),
        P(None, None, "grp", "dev", None),
        P(),
        P("grp", "dev", None),
    )
    out_specs = P(None, None, "grp", "dev", None)
    return jax.shard_map(shards, mesh=mesh, in_specs=in_specs, out_specs=out_specs, check_vma=False)
```

```python
import functools

import jax
import jax.numpy as jnp
import numpy as np
from jax import lax
from jax.experimental import pallas as pl
from jax.experimental.pallas import tpu as pltpu
from jax.sharding import PartitionSpec as P

DT = 0.08
LIFT = 6.0
NODE = (3, 4, 4, 4, 8, 128)
ROW = (6, 32, 8, 128)
FACE = 24
EXT = 2 * FACE
COEF = EXT + 3
STEP = {"dev": 1, "grp": 2}
LIMIT = 48 * 1024 * 1024


def gll_derivative():
    points = np.array([-1.0, -1.0 / np.sqrt(5.0), 1.0 / np.sqrt(5.0), 1.0])
    products = np.array(
        [
            np.prod([points[first] - points[second] for second in range(4) if second != first])
            for first in range(4)
        ]
    )
    matrix = np.zeros((4, 4))
    for first in range(4):
        for second in range(4):
            if first != second:
                matrix[first, second] = (
                    products[first] / products[second] / (points[first] - points[second])
                )
        matrix[first, first] = sum(
            (1.0 / (points[first] - points[other]) for other in range(4) if other != first)
        )
    return matrix


D = gll_derivative()
SCALE = [float(x) / 2 for x in (D[0, 0] + D[0, 3], D[0, 0] - D[0, 3], D[0, 1] - D[0, 2])]
RATIO = [float(x) / 2 / s for x, s in zip((D[1, 0] + D[1, 3], D[1, 0] - D[1, 3], D[1, 1] - D[1, 2]), SCALE)]


def roll(x, shift, axis):
    size = x.shape[axis]
    return pltpu.roll(x, shift % size, axis)


def sublane(shape):
    return lax.broadcasted_iota(jnp.int32, shape, len(shape) - 2)


def bit(shape, step):
    return (sublane(shape) & step) != 0


def even_device(axis):
    return lax.rem(lax.axis_index(axis), 2) == 0


def coefficients(speeds_ref, factor=1.0):
    out = []
    low_half = sublane((8, 128)) < 4
    for d in range(3):
        v = speeds_ref[pl.ds(8 * d, 8), :]
        w = roll(v, 4, 0)
        a = jnp.where(low_half, v, w)
        b = jnp.where(low_half, w, v)
        c = 0.5 * (a + b)
        dt = DT * factor
        out.append(
            (
                -dt * c,
                (-dt * LIFT) * (c - jnp.minimum(a, 0.0)),
                (dt * LIFT) * jnp.maximum(a, 0.0),
                (-dt * LIFT) * (jnp.maximum(b, 0.0) - c),
                (-dt * LIFT) * jnp.minimum(b, 0.0),
                (-dt * LIFT) * jnp.minimum(a, 0.0),
                (dt * LIFT) * jnp.maximum(b, 0.0),
            )
        )
    return out


def rim_coefficients(coef, step):
    upper = bit((8, 128), step)
    return jnp.where(upper, coef[4], coef[2]), jnp.where(upper, coef[6], coef[5])


def local(coef, step):
    c, low, low_in, high, high_in = coef[:5]
    if step:
        upper = bit((8, 128), step)
        low_in, high_in = jnp.where(upper, low_in, 0.0), jnp.where(upper, 0.0, high_in)
    return [c * s for s in SCALE], low, low_in, high, high_in, step


def line(q, c):
    t = c[0] * ((q[0] + q[3]) - (q[1] + q[2]))
    o0 = c[1] * (q[0] - q[3])
    o1 = c[2] * (q[1] - q[2])
    e = RATIO[0] * t
    o = RATIO[1] * o0 + RATIO[2] * o1
    o0 = o0 + o1
    return [o0 + t, o + e, o - e, o0 - t]


def beside_faces(q, coef):
    c, low, low_in, high, high_in, step = coef
    axis = q[0].ndim - 2 if step else q[0].ndim - 1
    step = step if step else 1
    r = line(q, c)
    r[0] = r[0] + low_in * roll(q[3], step, axis)
    r[3] = r[3] + high_in * roll(q[0], -step, axis)
    return r


def with_faces(q, coef):
    r = beside_faces(q, coef)
    r[0] = r[0] + coef[1] * q[0]
    r[3] = r[3] + coef[3] * q[3]
    return r


def own_terms(coef, keep):
    x, y, z = [[c[1], 0.0, 0.0, c[3]] for c in coef]
    x = jnp.stack([jnp.broadcast_to(keep + v, (8, 128)) for v in x])
    return [[x + (y[j] + z[k]) for j in range(4)] for k in range(4)]


def beside(low, high, halo_dn, halo_up, step):
    upper = bit(low.shape, step)
    dn = jnp.where(upper, roll(high, step, low.ndim - 2), halo_dn)
    up = jnp.where(upper, halo_up, roll(low, -step, low.ndim - 2))
    return dn, up


def pack_high(a, b, step):
    return jnp.where(bit(a.shape, step), b, roll(a, -step, a.ndim - 2))


def pack_low(a, b, step):
    return jnp.where(bit(a.shape, step), roll(a, step, a.ndim - 2), b)


def unpack_dn(m, second, step):
    return roll(m, -step, m.ndim - 2) if second else m


def unpack_up(m, second, step):
    return roll(m, step, m.ndim - 2) if second else m


def tendency(q_ref, acc_ref, p, along, own, finish, between=lambda step: None):
    for k in range(4):
        between(k)
        rx = beside_faces([q_ref[p, k, :, i] for i in range(4)], along[0])
        for i in range(4):
            acc_ref[p, k, :, i] = rx[i]
        ry = beside_faces([q_ref[p, k, j] for j in range(4)], along[1])
        for j in range(4):
            acc_ref[p, k, j] = acc_ref[p, k, j] + ry[j]
    for j in range(4):
        qz = [q_ref[p, k, j] for k in range(4)]
        rz = beside_faces(qz, along[2])
        for k in range(4):
            finish(p, k, j, acc_ref[p, k, j] + (rz[k] + own[k][j] * qz[k]))


def locals_of(coef):
    return [local(coef[d], d) for d in range(3)]


AXES = ("dev", "grp")
FIRST = (("dev", 1), ("dev", 0), ("grp", 1), ("grp", 0))
SECOND = (("dev", 1), ("dev", 0), ("grp", 1), ("grp", 0))


def put(messages, axis, at, to_next, to_last):
    even = even_device(axis)
    first, second = messages[axis, 0], messages[axis, 1]
    first[at] = jnp.where(even, to_next, to_last)
    second[at] = jnp.where(even, to_last, to_next)


def get(messages, axis, at):
    even = even_device(axis)
    first, second = messages[axis, 0], messages[axis, 1]
    x, y = first[at], second[at]
    return jnp.where(even, y, x), jnp.where(even, x, y)


def get_single(messages, axis, at, second):
    last, after = get(messages, axis, at)
    step = STEP[axis]
    return unpack_dn(last, second, step), unpack_up(after, second, step)


def face(q_ref, p, axis, side, plane):
    return q_ref[p, plane, side] if axis == "dev" else q_ref[p, side, plane]


def put_faces(q_ref, p, messages, base):
    for axis in AXES:
        step = STEP[axis]
        for half in range(2):
            m = 2 * half
            low = [face(q_ref, p, axis, 0, m + h) for h in range(2)]
            high = [face(q_ref, p, axis, 3, m + h) for h in range(2)]
            put(
                messages,
                axis,
                pl.ds(base + 8 * p + 4 * half, 4),
                pack_high(high[0], high[1], step),
                pack_low(low[0], low[1], step),
            )


def get_face(messages, axis, p, plane, base):
    at = pl.ds(base + 8 * p + 4 * (plane // 2), 4)
    return get_single(messages, axis, at, plane % 2)


def along_plane(h, along_x, along_t):
    out = with_faces(h, along_t)
    for t in range(4):
        out[t] = out[t] + jnp.stack(with_faces([h[t][i] for i in range(4)], along_x))
    return out


def across(coef, step):
    upper = bit((8, 128), step)
    c = jnp.where(upper, -coef[0], coef[0])
    out = [c * float(D[0, n]) for n in range(4)]
    out[0] = out[0] + jnp.where(upper, coef[3], coef[1])
    return out


def put_planes(planes, p, messages, base):
    for axis in AXES:
        step = STEP[axis]
        for half in range(2):
            a, b = planes[axis][2 * half : 2 * half + 2]
            at = pl.ds(base + 8 * p + 4 * half, 4)
            put(messages, axis, at, pack_high(a, b, step), pack_low(a, b, step))


def open_kernel(fields_hbm, speeds_hbm, count_hbm, *refs):
    q_ref, ext_ref, wide_count_ref, speeds_ref = refs[:4]
    messages, (fields_ref, count_ref, sems) = dict(zip(FIRST, refs[4:8])), refs[8:]
    copies = [
        pltpu.make_async_copy(speeds_hbm, speeds_ref, sems.at[3]),
        pltpu.make_async_copy(count_hbm, count_ref, sems.at[4]),
    ]

    def part(p):
        at = pl.ds(2 * p, 2)
        return pltpu.make_async_copy(fields_hbm.at[at], fields_ref.at[at], sems.at[p])

    for copy in copies + [part(p) for p in range(3)]:
        copy.start()
    for copy in copies:
        copy.wait()
    low_half = sublane((8, 128)) < 4
    coef = coefficients(speeds_ref)
    counts = count_ref[...].astype(jnp.float32)
    wide_count_ref[...] = jnp.concatenate([counts, counts], axis=0)
    for axis, d in (("dev", 2), ("grp", 1)):
        pair = rim_coefficients(coef[d], STEP[AXES[d - 1]])
        put(
            messages,
            axis,
            COEF,
            pack_high(pair[0], pair[1], STEP[axis]),
            pack_low(pair[0], pair[1], STEP[axis]),
        )

    along = locals_of(coef)
    across_y, across_z = across(coef[1], 1), across(coef[2], 2)
    high_y, high_z = bit((8, 128), 1), bit((8, 128), 2)

    def pair(p, carry):
        part(p).wait()
        tops, bottoms = [], []
        for k in range(4):
            for j in range(4):
                for h in range(2):
                    m = 8 * k + 2 * j + h
                    a = fields_ref[2 * p, m]
                    b = fields_ref[2 * p + 1, m]
                    x = jnp.where(low_half, a, roll(b, 4, 0))
                    y = jnp.where(low_half, roll(a, 4, 0), b)
                    q_ref[p, k, j, 2 * h] = x
                    q_ref[p, k, j, 2 * h + 1] = y
                    tops.append(jnp.maximum(x, y))
                    bottoms.append(jnp.minimum(x, y))
        while len(tops) > 1:
            tops = [jnp.maximum(x, y) for x, y in zip(tops[::2], tops[1::2])]
            bottoms = [jnp.minimum(x, y) for x, y in zip(bottoms[::2], bottoms[1::2])]
        ext_ref[0, p] = tops[0]
        ext_ref[1, p] = bottoms[0]
        for axis in AXES:
            put(
                messages,
                axis,
                EXT + p,
                pack_high(tops[0], bottoms[0], STEP[axis]),
                pack_low(tops[0], bottoms[0], STEP[axis]),
            )
        ys, zs = [], []
        for t in range(4):
            qy, qz = [q_ref[p, t, j] for j in range(4)], [q_ref[p, k, t] for k in range(4)]
            ys.append([jnp.where(high_y, qy[3 - n], qy[n]) for n in range(4)])
            zs.append([jnp.where(high_z, qz[3 - n], qz[n]) for n in range(4)])
        planes = {"dev": [y[0] for y in ys], "grp": [z[0] for z in zs]}
        put_planes(planes, p, messages, 0)
        later = {}
        for axis, lines, ways, other in (("dev", ys, across_y, along[2]), ("grp", zs, across_z, along[1])):
            tangent = along_plane(planes[axis], along[0], other)
            later[axis] = []
            for t in range(4):
                x = ways[0] * lines[t][0] + ways[1] * lines[t][1]
                x = x + (ways[2] * lines[t][2] + ways[3] * lines[t][3])
                later[axis].append(lines[t][0] + (tangent[t] + x))
        put_planes(later, p, messages, FACE)
        return carry

    lax.fori_loop(0, 3, pair, 0)


def bounds(ext_ref, messages, p):
    top, bottom = ext_ref[0, p], ext_ref[1, p]
    upper = jnp.maximum(top, jnp.maximum(roll(top, 1, 1), roll(top, -1, 1)))
    lower = jnp.minimum(bottom, jnp.minimum(roll(bottom, 1, 1), roll(bottom, -1, 1)))
    for axis in AXES:
        dn, up = beside(top, top, *get_single(messages, axis, EXT + p, 0), STEP[axis])
        upper = jnp.maximum(upper, jnp.maximum(dn, up))
        dn, up = beside(bottom, bottom, *get_single(messages, axis, EXT + p, 1), STEP[axis])
        lower = jnp.minimum(lower, jnp.minimum(dn, up))
    return upper, lower


def outer(pair, step):
    return jnp.where(bit(pair[0].shape, step), pair[1], pair[0])


def spread(coef, step):
    upper = bit((8, 128), step)
    c, low, _, high = coef[:4]
    out = [c * jnp.where(upper, float(D[n, 3]), float(D[n, 0])) for n in range(4)]
    out[0] = out[0] + jnp.where(upper, 0.0, low)
    out[3] = out[3] + jnp.where(upper, high, 0.0)
    return out


def local_kernel(q_ref, speeds_ref, sharpen_ref, out_ref, both_ref, rim_ref, part_ref):
    coef = coefficients(speeds_ref)
    some = coefficients(speeds_ref, 0.25)
    build_operators(sharpen_ref, both_ref, rim_ref)

    own, own_some = own_terms(coef, 1.0), own_terms(some, 0.25)
    along, along_some = locals_of(coef), locals_of(some)

    def middle(p, k, j, t):
        part_ref[p, k, j] = t

    def finish(p, k, j, t):
        out_ref[p, k, j] = 0.75 * q_ref[p, k, j] + t

    def pair(p, carry):
        tendency(q_ref, part_ref, p, along, own, middle)
        tendency(part_ref, out_ref, p, along_some, own_some, finish)
        return carry

    lax.fori_loop(0, 3, pair, 0)


def first_kernel(q_ref, base_ref, speeds_ref, *refs):
    got, messages = dict(zip(FIRST, refs[:4])), dict(zip(SECOND, refs[7:]))
    out_ref, corner_ref, weight_ref = refs[4:7]
    coef = coefficients(speeds_ref)
    in_y, to_y = rim_coefficients(coef[1], 1)
    in_z, to_z = rim_coefficients(coef[2], 2)
    in_zn, to_zn = [outer(get_single(got, "dev", COEF, h), 1) for h in range(2)]
    in_ym, to_ym = [outer(get_single(got, "grp", COEF, h), 2) for h in range(2)]
    weight_ref[...] = 0.25 * (in_y * in_zn + in_z * in_ym)
    weight_n = 0.25 * (to_y * in_z + in_zn * to_ym)
    weight_m = 0.25 * (to_z * in_y + in_ym * to_zn)
    high_y, high_z = bit((8, 128), 1), bit((8, 128), 2)
    some_y, some_z = 0.25 * in_y, 0.25 * in_z
    along = locals_of(coef)
    spread_y, spread_z = spread(coef[1], 1), spread(coef[2], 2)

    def pair(p, carry):
        from_n = [outer(get_face(got, "dev", p, k, 0), 1) for k in range(4)]
        from_m = [outer(get_face(got, "grp", p, j, 0), 2) for j in range(4)]
        edge_n = jnp.where(high_z, from_n[3], from_n[0])
        edge_m = jnp.where(high_y, from_m[3], from_m[0])
        corner_ref[0, p] = weight_n * edge_m
        corner_ref[1, p] = weight_m * edge_n
        put(
            messages,
            "dev",
            pl.ds(FACE + 2 * p, 2),
            pack_high(edge_m[:2], edge_m[2:], 1),
            pack_low(edge_m[:2], edge_m[2:], 1),
        )
        hy = [some_y * x for x in from_n]
        hz = [some_z * x for x in from_m]
        plane_y = along_plane(hy, along[0], along[2])
        plane_z = along_plane(hz, along[0], along[1])
        for n in range(4):
            own = jnp.where(high_y, q_ref[p, n, 3], q_ref[p, n, 0])
            ghost = outer(get_face(got, "dev", p, n, FACE), 1) + to_y * own
            plane_y[n] = plane_y[n] + (hy[n] + some_y * ghost)
            own = jnp.where(high_z, q_ref[p, 3, n], q_ref[p, 0, n])
            ghost = outer(get_face(got, "grp", p, n, FACE), 2) + to_z * own
            plane_z[n] = plane_z[n] + (hz[n] + some_z * ghost)
        for k in range(4):
            for j in range(4):
                value = base_ref[p, k, j] + (spread_y[j] * hy[k] + spread_z[k] * hz[j])
                if j in (0, 3):
                    value = value + jnp.where(high_y == (j == 3), plane_y[k], 0.0)
                if k in (0, 3):
                    value = value + jnp.where(high_z == (k == 3), plane_z[j], 0.0)
                out_ref[p, k, j] = value
        put_faces(out_ref, p, messages, 0)
        return carry

    lax.fori_loop(0, 3, pair, 0)


def build_operators(sharpen_ref, both_ref, rim_ref):
    f32, bf16 = jnp.float32, jnp.bfloat16

    def index(shape, axis):
        return lax.broadcasted_iota(jnp.int32, shape, axis)

    tall = (index((256, 64), 0) // 4 == index((256, 64), 1)).astype(bf16)
    wide = (index((64, 256), 1) // 4 == index((64, 256), 0)).astype(f32)
    node, col = index((64, 128), 0), index((64, 128), 1)
    t, i = (col >> 4) & 3, (col >> 2) & 3
    on_y = 16 * t + 12 * (col & 1) + i
    on_z = 48 * ((col >> 1) & 1) + 4 * t + i
    pick = (node == jnp.where(col < 64, on_y, on_z)).astype(f32)
    wide = jnp.concatenate([wide, pick], axis=1).astype(bf16)
    same = (index((256, 128), 0) & 3) == (index((256, 128), 1) & 3)
    for n, part in enumerate(split(sharpen_ref[...])):
        half = jnp.dot(tall, part, preferred_element_type=f32).astype(bf16)
        full = jnp.dot(half, wide, preferred_element_type=f32)
        full = [jnp.where(same, full[:, 128 * m : 128 * m + 128], 0.0).astype(bf16) for m in range(3)]
        at = pl.ds(256 * n, 256)
        both_ref[at, :] = jnp.concatenate(full[:2], axis=1)
        rim_ref[at, :] = jnp.concatenate([full[2], full[2]], axis=1)


def split(x):
    high = x.astype(jnp.bfloat16)
    return high, (x - high.astype(jnp.float32)).astype(jnp.bfloat16)


def to_rows(pairs):
    low_half = sublane((8, 128)) < 4
    rows = []
    for x, y in pairs:
        rows.append(jnp.where(low_half, x, roll(y, 4, 0)))
        rows.append(jnp.where(low_half, roll(x, 4, 0), y))
    return rows


def presence(count_ref):
    counts = count_ref[...]
    return [(counts > float(f)).astype(jnp.float32) for f in range(6)], 1.0 / counts


def offsets(rows, present, share):
    mean = rows[0] * present[0]
    for f in range(1, 6):
        mean = mean + rows[f] * present[f]
    mean = mean * share
    return [(rows[f] - mean) * present[f] for f in range(6)]


def columns(ref, p, rows):
    return jnp.concatenate([ref[2 * p].reshape(rows, 128), ref[2 * p + 1].reshape(rows, 128)], axis=1)


def inner_kernel(q_ref, part_ref, speeds_ref, ext_ref, count_ref, both_ref, *refs):
    got, (out_ref, limit_ref, acc_ref, fix_ref) = dict(zip(FIRST, refs[:4])), refs[4:]
    coef = coefficients(speeds_ref, 2.0 / 3.0)
    low_half = sublane((8, 128)) < 4

    own, along = own_terms(coef, 2.0 / 3.0), locals_of(coef)

    def finish(p, k, j, t):
        acc_ref[p, k, j] = (1.0 / 3.0) * q_ref[p, k, j] + t

    def product(p, step=2):
        if p < 0 or step != 2:
            return
        both = both_ref[...]
        x_high, x_low = parts[p]
        fix = jnp.dot(both, x_high, preferred_element_type=jnp.float32)
        fix = fix[:256] + fix[256:] + jnp.dot(both[:256], x_low, preferred_element_type=jnp.float32)
        for h in range(2):
            fix_ref[2 * p + h] = fix[:, 128 * h : 128 * h + 128].reshape(32, 8, 128)

    parts = []
    for p in range(3):
        tendency(part_ref, acc_ref, p, along, own, finish, functools.partial(product, p - 1))
        for n in range(32):
            k, j, h = n // 8, n // 2 % 4, n % 2
            rows = to_rows([(acc_ref[p, k, j, 2 * h], acc_ref[p, k, j, 2 * h + 1])])
            out_ref[2 * p, n], out_ref[2 * p + 1, n] = rows
        parts.append(split(columns(out_ref, p, 256)))
        for n, x in enumerate(bounds(ext_ref, got, p)):
            y = roll(x, 4, 0)
            limit_ref[n, 2 * p] = jnp.where(low_half, x, y)
            limit_ref[n, 2 * p + 1] = jnp.where(low_half, y, x)
    product(2)
    present, share = presence(count_ref)
    for n in range(32):
        off = offsets([fix_ref[f, n] for f in range(6)], present, share)
        for f in range(6):
            out_ref[f, n] = out_ref[f, n] + off[f]


def last_kernel(
    base_ref, speeds_ref, limit_ref, corner_ref, weight_ref, count_ref, rim_ref, *refs
):
    got, out_hbm = dict(zip(SECOND, refs[:4])), refs[4]
    plane_ref, off_ref, out_ref, sems = refs[5:]

    def part(p):
        at = pl.ds(2 * p, 2)
        return pltpu.make_async_copy(out_ref.at[at], out_hbm.at[at], sems.at[p])

    coef = coefficients(speeds_ref)
    in_y, _ = rim_coefficients(coef[1], 1)
    in_z, _ = rim_coefficients(coef[2], 2)
    high_y, high_z = bit((8, 128), 1), bit((8, 128), 2)
    some_y, some_z = (2.0 / 3.0) * in_y, (2.0 / 3.0) * in_z
    spread_y, spread_z = spread(coef[1], 1), spread(coef[2], 2)
    weight = (2.0 / 3.0) * weight_ref[...]
    present, share = presence(count_ref)

    planes = []
    for p in range(3):
        at = pl.ds(FACE + 2 * p, 2)
        late = weight * jnp.concatenate(
            [outer(get_single(got, "dev", at, h), 1) for h in range(2)], axis=0
        )
        x = with_faces([late[i] for i in range(4)], local(coef[0], 0))
        at_corner = late + jnp.stack(x) + some_y * corner_ref[0, p]
        to_corner = some_z * corner_ref[1, p]
        both = []
        for k in range(4):
            value = some_y * outer(get_face(got, "dev", p, k, 0), 1) + spread_z[k] * late
            if k in (0, 3):
                value = value + jnp.where(high_z == (k == 3), at_corner, 0.0)
            both.append(value)
        for j in range(4):
            value = some_z * outer(get_face(got, "grp", p, j, 0), 2) + spread_y[j] * late
            if j in (0, 3):
                value = value + jnp.where(high_y == (j == 3), to_corner, 0.0)
            both.append(value)
        planes.append(both)
    for t in range(8):
        for h in range(2):
            rows = to_rows([(planes[p][t][2 * h], planes[p][t][2 * h + 1]) for p in range(3)])
            off = offsets(rows, present, share)
            for f in range(6):
                plane_ref[f, 2 * t + h] = rows[f]
                off_ref[f, 2 * t + h] = off[f]

    rim = rim_ref[...]
    for p in range(3):
        off_high, off_low = split(columns(off_ref, p, 128))
        fix = jnp.dot(rim, jnp.concatenate([off_high, off_low], axis=0), preferred_element_type=jnp.float32)
        fix = fix[:256] + fix[256:]
        for g in range(2):
            f = 2 * p + g
            part_fix = fix[:, 128 * g : 128 * g + 128].reshape(4, 4, 2, 8, 128)
            for k in range(4):
                for j in range(4):
                    at = pl.ds(8 * k + 2 * j, 2)
                    value = base_ref[f, at] + part_fix[k, j]
                    if j in (0, 3):
                        value = value + jnp.where(high_y == (j == 3), plane_ref[f, pl.ds(2 * k, 2)], 0.0)
                    if k in (0, 3):
                        value = value + jnp.where(
                            high_z == (k == 3), plane_ref[f, pl.ds(8 + 2 * j, 2)], 0.0
                        )
                    out_ref[f, at] = jnp.minimum(jnp.maximum(value, limit_ref[1, f]), limit_ref[0, f])
        part(p).start()
    for p in range(3):
        part(p).wait()


def call(kernel, outs, args, scratch=(), flops=5_000_000, space=pltpu.VMEM, out_space=pltpu.VMEM):
    return pl.pallas_call(
        kernel,
        out_shape=[jax.ShapeDtypeStruct(*o) for o in outs],
        in_specs=[pl.BlockSpec(memory_space=space)] * len(args),
        out_specs=[pl.BlockSpec(memory_space=out_space)] * len(outs),
        scratch_shapes=[pltpu.VMEM(*s) if isinstance(s, tuple) else s for s in scratch],
        compiler_params=pltpu.CompilerParams(vmem_limit_bytes=LIMIT),
        cost_estimate=pl.CostEstimate(flops=flops, bytes_accessed=2_000_000, transcendentals=0),
    )(*args)


EVEN_PAIRS = [(i, i ^ 1) for i in range(16)]
ODD_PAIRS = [((i + 1) % 16, ((i ^ 1) + 1) % 16) for i in range(16)]


def exchange(messages, ways):
    pairs = (EVEN_PAIRS, ODD_PAIRS)
    return [lax.ppermute(m, axis, pairs[odd]) for m, (axis, odd) in zip(messages, ways)]


def shards(fields, speeds, sharpen, mat_count):
    f32, bf16 = jnp.float32, jnp.bfloat16
    rows = fields.reshape(ROW)
    speeds = speeds.reshape(24, 128)
    counts = mat_count.reshape(4, 128)
    node, one, ext = (NODE, f32), ((8, 128), f32), ((2, 3, 8, 128), f32)
    corner = ((2, 3, 4, 8, 128), f32)
    q, extremes, counts, speeds, *messages = call(
        open_kernel,
        [node, ext, one, ((24, 128), f32)] + [((COEF + 1, 8, 128), f32)] * 4,
        [pltpu.with_memory_space_constraint(x, pltpu.HBM) for x in (rows, speeds, counts)],
        scratch=[(ROW, f32), ((4, 128), jnp.int32), pltpu.SemaphoreType.DMA((5,))],
        space=pltpu.HBM,
    )
    first = exchange(messages, FIRST)
    tall = ((512, 256), bf16)
    base, both, rim = call(local_kernel, [node, tall, tall], [q, speeds, sharpen], scratch=[node])
    s, corners, weight, *messages = call(
        first_kernel,
        [node, corner, one] + [((FACE + (6 if axis == "dev" else 0), 8, 128), f32) for axis, _ in SECOND],
        [q, base, speeds, *first],
    )
    second = exchange(messages, SECOND)
    base, limits = call(
        inner_kernel,
        [(ROW, f32), ((2, 6, 8, 128), f32)],
        [q, s, speeds, extremes, counts, both, *first],
        scratch=[node, (ROW, f32)],
    )
    plane = ((6, 16, 8, 128), f32)
    (out,) = call(
        last_kernel,
        [(ROW, f32)],
        [base, speeds, limits, corners, weight, counts, rim, *second],
        scratch=[plane, plane, (ROW, f32), pltpu.SemaphoreType.DMA((3,))],
        out_space=pltpu.HBM,
    )
    return out.reshape(fields.shape)


def solution(mesh):
    in_specs = (
        P(None, None, "grp", "dev", None),
        P(None, None, "grp", "dev", None),
        P(),
        P("grp", "dev", None),
    )
    out_specs = P(None, None, "grp", "dev", None)
    return jax.shard_map(shards, mesh=mesh, in_specs=in_specs, out_specs=out_specs, check_vma=False)
```

```python
import functools

import jax
import jax.numpy as jnp
import numpy as np
from jax import lax
from jax.experimental import pallas as pl
from jax.experimental.pallas import tpu as pltpu
from jax.sharding import PartitionSpec as P

DT = 0.08
LIFT = 6.0
NODE = (3, 4, 4, 4, 8, 128)
ROW = (6, 32, 8, 128)
FACE = 24
COEF = 2 * FACE
EXT = {"dev": FACE + 6, "grp": FACE}
STEP = {"dev": 1, "grp": 2}
LIMIT = 48 * 1024 * 1024


def gll_derivative():
    points = np.array([-1.0, -1.0 / np.sqrt(5.0), 1.0 / np.sqrt(5.0), 1.0])
    products = np.array(
        [
            np.prod([points[first] - points[second] for second in range(4) if second != first])
            for first in range(4)
        ]
    )
    matrix = np.zeros((4, 4))
    for first in range(4):
        for second in range(4):
            if first != second:
                matrix[first, second] = (
                    products[first] / products[second] / (points[first] - points[second])
                )
        matrix[first, first] = sum(
            (1.0 / (points[first] - points[other]) for other in range(4) if other != first)
        )
    return matrix


D = gll_derivative()
SCALE = [float(x) / 2 for x in (D[0, 0] + D[0, 3], D[0, 0] - D[0, 3], D[0, 1] - D[0, 2])]
RATIO = [float(x) / 2 / s for x, s in zip((D[1, 0] + D[1, 3], D[1, 0] - D[1, 3], D[1, 1] - D[1, 2]), SCALE)]


def roll(x, shift, axis):
    size = x.shape[axis]
    return pltpu.roll(x, shift % size, axis)


def sublane(shape):
    return lax.broadcasted_iota(jnp.int32, shape, len(shape) - 2)


def bit(shape, step):
    return (sublane(shape) & step) != 0


def even_device(axis):
    return lax.rem(lax.axis_index(axis), 2) == 0


def coefficients(speeds_ref, factor=1.0):
    out = []
    low_half = sublane((8, 128)) < 4
    for d in range(3):
        v = speeds_ref[pl.ds(8 * d, 8), :]
        w = roll(v, 4, 0)
        a = jnp.where(low_half, v, w)
        b = jnp.where(low_half, w, v)
        c = 0.5 * (a + b)
        dt = DT * factor
        out.append(
            (
                -dt * c,
                (-dt * LIFT) * (c - jnp.minimum(a, 0.0)),
                (dt * LIFT) * jnp.maximum(a, 0.0),
                (-dt * LIFT) * (jnp.maximum(b, 0.0) - c),
                (-dt * LIFT) * jnp.minimum(b, 0.0),
                (-dt * LIFT) * jnp.minimum(a, 0.0),
                (dt * LIFT) * jnp.maximum(b, 0.0),
            )
        )
    return out


def rim_coefficients(coef, step):
    upper = bit((8, 128), step)
    return jnp.where(upper, coef[4], coef[2]), jnp.where(upper, coef[6], coef[5])


def local(coef, step):
    c, low, low_in, high, high_in = coef[:5]
    if step:
        upper = bit((8, 128), step)
        low_in, high_in = jnp.where(upper, low_in, 0.0), jnp.where(upper, 0.0, high_in)
    return [c * s for s in SCALE], low, low_in, high, high_in, step


def line(q, c):
    t = c[0] * ((q[0] + q[3]) - (q[1] + q[2]))
    o0 = c[1] * (q[0] - q[3])
    o1 = c[2] * (q[1] - q[2])
    e = RATIO[0] * t
    o = RATIO[1] * o0 + RATIO[2] * o1
    o0 = o0 + o1
    return [o0 + t, o + e, o - e, o0 - t]


def beside_faces(q, coef):
    c, low, low_in, high, high_in, step = coef
    axis = q[0].ndim - 2 if step else q[0].ndim - 1
    step = step if step else 1
    r = line(q, c)
    r[0] = r[0] + low_in * roll(q[3], step, axis)
    r[3] = r[3] + high_in * roll(q[0], -step, axis)
    return r


def with_faces(q, coef):
    r = beside_faces(q, coef)
    r[0] = r[0] + coef[1] * q[0]
    r[3] = r[3] + coef[3] * q[3]
    return r


def own_terms(coef, keep):
    x, y, z = [[c[1], 0.0, 0.0, c[3]] for c in coef]
    x = jnp.stack([jnp.broadcast_to(keep + v, (8, 128)) for v in x])
    return [[x + (y[j] + z[k]) for j in range(4)] for k in range(4)]


def beside(low, high, halo_dn, halo_up, step):
    upper = bit(low.shape, step)
    dn = jnp.where(upper, roll(high, step, low.ndim - 2), halo_dn)
    up = jnp.where(upper, halo_up, roll(low, -step, low.ndim - 2))
    return dn, up


def pack_high(a, b, step):
    return jnp.where(bit(a.shape, step), b, roll(a, -step, a.ndim - 2))


def pack_low(a, b, step):
    return jnp.where(bit(a.shape, step), roll(a, step, a.ndim - 2), b)


def unpack_dn(m, second, step):
    return roll(m, -step, m.ndim - 2) if second else m


def unpack_up(m, second, step):
    return roll(m, step, m.ndim - 2) if second else m


def tendency(q_ref, acc_ref, p, along, own, finish, between=lambda step: None):
    for k in range(4):
        between(k)
        rx = beside_faces([q_ref[p, k, :, i] for i in range(4)], along[0])
        for i in range(4):
            acc_ref[p, k, :, i] = rx[i]
        ry = beside_faces([q_ref[p, k, j] for j in range(4)], along[1])
        for j in range(4):
            acc_ref[p, k, j] = acc_ref[p, k, j] + ry[j]
    for j in range(4):
        qz = [q_ref[p, k, j] for k in range(4)]
        rz = beside_faces(qz, along[2])
        for k in range(4):
            finish(p, k, j, acc_ref[p, k, j] + (rz[k] + own[k][j] * qz[k]))


def locals_of(coef):
    return [local(coef[d], d) for d in range(3)]


AXES = ("dev", "grp")
FIRST = (("dev", 1), ("dev", 0), ("grp", 1), ("grp", 0))
SECOND = (("dev", 1), ("dev", 0), ("grp", 1), ("grp", 0))


def put(messages, axis, at, to_next, to_last):
    even = even_device(axis)
    first, second = messages[axis, 0], messages[axis, 1]
    first[at] = jnp.where(even, to_next, to_last)
    second[at] = jnp.where(even, to_last, to_next)


def get_outer(messages, axis, at, second):
    step, even = STEP[axis], even_device(axis)
    first, other = messages[axis, 0][at], messages[axis, 1][at]
    upper = bit(first.shape, step)
    here = upper == even
    if not second:
        return jnp.where(here, first, other)
    there = jnp.where(here, other, first)
    dim = first.ndim - 2
    return jnp.where(upper, roll(there, step, dim), roll(there, -step, dim))


def face(q_ref, p, axis, side, plane):
    return q_ref[p, plane, side] if axis == "dev" else q_ref[p, side, plane]


def put_faces(q_ref, p, messages, base):
    for axis in AXES:
        step = STEP[axis]
        for half in range(2):
            m = 2 * half
            low = [face(q_ref, p, axis, 0, m + h) for h in range(2)]
            high = [face(q_ref, p, axis, 3, m + h) for h in range(2)]
            put(
                messages,
                axis,
                pl.ds(base + 8 * p + 4 * half, 4),
                pack_high(high[0], high[1], step),
                pack_low(low[0], low[1], step),
            )


def get_face(messages, axis, p, plane, base):
    at = pl.ds(base + 8 * p + 4 * (plane // 2), 4)
    return get_outer(messages, axis, at, plane % 2)


def along_plane(h, along_x, along_t):
    out = with_faces(h, along_t)
    for t in range(4):
        out[t] = out[t] + jnp.stack(with_faces([h[t][i] for i in range(4)], along_x))
    return out


def across(coef, step):
    upper = bit((8, 128), step)
    c = jnp.where(upper, -coef[0], coef[0])
    out = [c * float(D[0, n]) for n in range(4)]
    out[0] = out[0] + jnp.where(upper, coef[3], coef[1])
    return out


def put_planes(planes, p, messages, base):
    for axis in AXES:
        step = STEP[axis]
        for half in range(2):
            a, b = planes[axis][2 * half : 2 * half + 2]
            at = pl.ds(base + 8 * p + 4 * half, 4)
            put(messages, axis, at, pack_high(a, b, step), pack_low(a, b, step))


def open_kernel(fields_hbm, speeds_hbm, count_hbm, *refs):
    q_ref, wide_count_ref, speeds_ref = refs[:3]
    messages, (fields_ref, count_ref, sems) = dict(zip(FIRST, refs[3:7])), refs[7:]
    copies = [
        pltpu.make_async_copy(speeds_hbm, speeds_ref, sems.at[3]),
        pltpu.make_async_copy(count_hbm, count_ref, sems.at[4]),
    ]

    def part(p):
        at = pl.ds(2 * p, 2)
        return pltpu.make_async_copy(fields_hbm.at[at], fields_ref.at[at], sems.at[p])

    for copy in copies + [part(p) for p in range(3)]:
        copy.start()
    for copy in copies:
        copy.wait()
    low_half = sublane((8, 128)) < 4
    coef = coefficients(speeds_ref)
    counts = count_ref[...].astype(jnp.float32)
    wide_count_ref[...] = jnp.concatenate([counts, counts], axis=0)
    for axis, d in (("dev", 2), ("grp", 1)):
        pair = rim_coefficients(coef[d], STEP[AXES[d - 1]])
        put(
            messages,
            axis,
            COEF,
            pack_high(pair[0], pair[1], STEP[axis]),
            pack_low(pair[0], pair[1], STEP[axis]),
        )

    along = locals_of(coef)
    across_y, across_z = across(coef[1], 1), across(coef[2], 2)
    high_y, high_z = bit((8, 128), 1), bit((8, 128), 2)

    def pair(p, carry):
        part(p).wait()
        for k in range(4):
            for j in range(4):
                for h in range(2):
                    m = 8 * k + 2 * j + h
                    a = fields_ref[2 * p, m]
                    b = fields_ref[2 * p + 1, m]
                    x = jnp.where(low_half, a, roll(b, 4, 0))
                    y = jnp.where(low_half, roll(a, 4, 0), b)
                    q_ref[p, k, j, 2 * h] = x
                    q_ref[p, k, j, 2 * h + 1] = y
        ys, zs = [], []
        for t in range(4):
            qy, qz = [q_ref[p, t, j] for j in range(4)], [q_ref[p, k, t] for k in range(4)]
            ys.append([jnp.where(high_y, qy[3 - n], qy[n]) for n in range(4)])
            zs.append([jnp.where(high_z, qz[3 - n], qz[n]) for n in range(4)])
        planes = {"dev": [y[0] for y in ys], "grp": [z[0] for z in zs]}
        put_planes(planes, p, messages, 0)
        later = {}
        for axis, lines, ways, other in (("dev", ys, across_y, along[2]), ("grp", zs, across_z, along[1])):
            tangent = along_plane(planes[axis], along[0], other)
            later[axis] = []
            for t in range(4):
                x = ways[0] * lines[t][0] + ways[1] * lines[t][1]
                x = x + (ways[2] * lines[t][2] + ways[3] * lines[t][3])
                later[axis].append(lines[t][0] + (tangent[t] + x))
        put_planes(later, p, messages, FACE)
        return carry

    lax.fori_loop(0, 3, pair, 0)


def bounds(ext_ref, p):
    out = []
    for x, most in ((ext_ref[0, p], jnp.maximum), (ext_ref[1, p], jnp.minimum)):
        y = most(x, most(roll(x, 1, 1), roll(x, -1, 1)))
        for step in (1, 2):
            y = most(y, jnp.where(bit(x.shape, step), roll(x, step, 0), roll(x, -step, 0)))
        out.append(y)
    return out


def spread(coef, step):
    upper = bit((8, 128), step)
    c, low, _, high = coef[:4]
    out = [c * jnp.where(upper, float(D[n, 3]), float(D[n, 0])) for n in range(4)]
    out[0] = out[0] + jnp.where(upper, 0.0, low)
    out[3] = out[3] + jnp.where(upper, high, 0.0)
    return out


def local_kernel(q_ref, speeds_ref, sharpen_ref, out_ref, ext_ref, both_ref, rim_ref, part_ref):
    coef = coefficients(speeds_ref)
    some = coefficients(speeds_ref, 0.25)
    build_operators(sharpen_ref, both_ref, rim_ref)

    own, own_some = own_terms(coef, 1.0), own_terms(some, 0.25)
    along, along_some = locals_of(coef), locals_of(some)

    def middle(p, k, j, t):
        part_ref[p, k, j] = t

    def finish(p, k, j, t):
        out_ref[p, k, j] = 0.75 * q_ref[p, k, j] + t

    def pair(p, carry):
        tops = [q_ref[p, k] for k in range(4)]
        bottoms = tops
        for _ in range(2):
            tops = [jnp.maximum(x, y) for x, y in zip(tops[::2], tops[1::2])]
            bottoms = [jnp.minimum(x, y) for x, y in zip(bottoms[::2], bottoms[1::2])]
        ext_ref[0, p] = jnp.max(tops[0].reshape(16, 8, 128), axis=0)
        ext_ref[1, p] = jnp.min(bottoms[0].reshape(16, 8, 128), axis=0)
        tendency(q_ref, part_ref, p, along, own, middle)
        tendency(part_ref, out_ref, p, along_some, own_some, finish)
        return carry

    lax.fori_loop(0, 3, pair, 0)


def first_kernel(q_ref, base_ref, speeds_ref, ext_ref, *refs):
    got, messages = dict(zip(FIRST, refs[:4])), dict(zip(SECOND, refs[7:]))
    out_ref, corner_ref, weight_ref = refs[4:7]
    coef = coefficients(speeds_ref)
    in_y, to_y = rim_coefficients(coef[1], 1)
    in_z, to_z = rim_coefficients(coef[2], 2)
    in_zn, to_zn = [get_outer(got, "dev", COEF, h) for h in range(2)]
    in_ym, to_ym = [get_outer(got, "grp", COEF, h) for h in range(2)]
    weight_ref[...] = 0.25 * (in_y * in_zn + in_z * in_ym)
    weight_n = 0.25 * (to_y * in_z + in_zn * to_ym)
    weight_m = 0.25 * (to_z * in_y + in_ym * to_zn)
    high_y, high_z = bit((8, 128), 1), bit((8, 128), 2)
    some_y, some_z = 0.25 * in_y, 0.25 * in_z
    along = locals_of(coef)
    spread_y, spread_z = spread(coef[1], 1), spread(coef[2], 2)

    def pair(p, carry):
        from_n = [get_face(got, "dev", p, k, 0) for k in range(4)]
        from_m = [get_face(got, "grp", p, j, 0) for j in range(4)]
        edge_n = jnp.where(high_z, from_n[3], from_n[0])
        edge_m = jnp.where(high_y, from_m[3], from_m[0])
        corner_ref[0, p] = weight_n * edge_m
        corner_ref[1, p] = weight_m * edge_n
        put(
            messages,
            "dev",
            pl.ds(FACE + 2 * p, 2),
            pack_high(edge_m[:2], edge_m[2:], 1),
            pack_low(edge_m[:2], edge_m[2:], 1),
        )
        hy = [some_y * x for x in from_n]
        hz = [some_z * x for x in from_m]
        plane_y = along_plane(hy, along[0], along[2])
        plane_z = along_plane(hz, along[0], along[1])
        for n in range(4):
            own = jnp.where(high_y, q_ref[p, n, 3], q_ref[p, n, 0])
            ghost = get_face(got, "dev", p, n, FACE) + to_y * own
            plane_y[n] = plane_y[n] + (hy[n] + some_y * ghost)
            own = jnp.where(high_z, q_ref[p, 3, n], q_ref[p, 0, n])
            ghost = get_face(got, "grp", p, n, FACE) + to_z * own
            plane_z[n] = plane_z[n] + (hz[n] + some_z * ghost)
        for k in range(4):
            for j in range(4):
                value = base_ref[p, k, j] + (spread_y[j] * hy[k] + spread_z[k] * hz[j])
                if j in (0, 3):
                    value = value + jnp.where(high_y == (j == 3), plane_y[k], 0.0)
                if k in (0, 3):
                    value = value + jnp.where(high_z == (k == 3), plane_z[j], 0.0)
                out_ref[p, k, j] = value
        put_faces(out_ref, p, messages, 0)
        for axis in AXES:
            step, pair = STEP[axis], (ext_ref[0, p], ext_ref[1, p])
            put(messages, axis, EXT[axis] + p, pack_high(*pair, step), pack_low(*pair, step))
        return carry

    lax.fori_loop(0, 3, pair, 0)


def build_operators(sharpen_ref, both_ref, rim_ref):
    f32, bf16 = jnp.float32, jnp.bfloat16

    def index(shape, axis):
        return lax.broadcasted_iota(jnp.int32, shape, axis)

    tall = (index((256, 64), 0) // 4 == index((256, 64), 1)).astype(bf16)
    wide = (index((64, 256), 1) // 4 == index((64, 256), 0)).astype(f32)
    node, col = index((64, 128), 0), index((64, 128), 1)
    t, i = (col >> 4) & 3, (col >> 2) & 3
    on_y = 16 * t + 12 * (col & 1) + i
    on_z = 48 * ((col >> 1) & 1) + 4 * t + i
    pick = (node == jnp.where(col < 64, on_y, on_z)).astype(f32)
    wide = jnp.concatenate([wide, pick], axis=1).astype(bf16)
    same = (index((256, 128), 0) & 3) == (index((256, 128), 1) & 3)
    for n, part in enumerate(split(sharpen_ref[...])):
        half = jnp.dot(tall, part, preferred_element_type=f32).astype(bf16)
        full = jnp.dot(half, wide, preferred_element_type=f32)
        full = [jnp.where(same, full[:, 128 * m : 128 * m + 128], 0.0).astype(bf16) for m in range(3)]
        at = pl.ds(256 * n, 256)
        both_ref[at, :] = jnp.concatenate(full[:2], axis=1)
        rim_ref[at, :] = jnp.concatenate([full[2], full[2]], axis=1)


def split(x):
    high = x.astype(jnp.bfloat16)
    return high, (x - high.astype(jnp.float32)).astype(jnp.bfloat16)


def to_rows(pairs):
    low_half = sublane((8, 128)) < 4
    rows = []
    for x, y in pairs:
        rows.append(jnp.where(low_half, x, roll(y, 4, 0)))
        rows.append(jnp.where(low_half, roll(x, 4, 0), y))
    return rows


def presence(count_ref):
    counts = count_ref[...]
    return [(counts > float(f)).astype(jnp.float32) for f in range(6)], 1.0 / counts


def offsets(rows, present, share):
    mean = rows[0] * present[0]
    for f in range(1, 6):
        mean = mean + rows[f] * present[f]
    mean = mean * share
    return [(rows[f] - mean) * present[f] for f in range(6)]


def columns(ref, p, rows):
    return jnp.concatenate([ref[2 * p].reshape(rows, 128), ref[2 * p + 1].reshape(rows, 128)], axis=1)


def inner_kernel(
    q_ref, part_ref, speeds_ref, ext_ref, count_ref, both_ref, out_ref, limit_ref, acc_ref, fix_ref
):
    coef = coefficients(speeds_ref, 2.0 / 3.0)
    low_half = sublane((8, 128)) < 4

    own, along = own_terms(coef, 2.0 / 3.0), locals_of(coef)

    def finish(p, k, j, t):
        acc_ref[p, k, j] = (1.0 / 3.0) * q_ref[p, k, j] + t

    def product(p, step=2):
        if p < 0 or step != 2:
            return
        both = both_ref[...]
        x_high, x_low = parts[p]
        fix = jnp.dot(both, x_high, preferred_element_type=jnp.float32)
        fix = fix[:256] + fix[256:] + jnp.dot(both[:256], x_low, preferred_element_type=jnp.float32)
        for h in range(2):
            fix_ref[2 * p + h] = fix[:, 128 * h : 128 * h + 128].reshape(32, 8, 128)

    parts = []
    for p in range(3):
        tendency(part_ref, acc_ref, p, along, own, finish, functools.partial(product, p - 1))
        for n in range(32):
            k, j, h = n // 8, n // 2 % 4, n % 2
            rows = to_rows([(acc_ref[p, k, j, 2 * h], acc_ref[p, k, j, 2 * h + 1])])
            out_ref[2 * p, n], out_ref[2 * p + 1, n] = rows
        parts.append(split(columns(out_ref, p, 256)))
        limit_ref[0, p], limit_ref[1, p] = bounds(ext_ref, p)
    product(2)
    present, share = presence(count_ref)
    for n in range(32):
        off = offsets([fix_ref[f, n] for f in range(6)], present, share)
        for f in range(6):
            out_ref[f, n] = out_ref[f, n] + off[f]


def last_kernel(
    base_ref, speeds_ref, limit_ref, corner_ref, weight_ref, count_ref, rim_ref, *refs
):
    got, out_hbm = dict(zip(SECOND, refs[:4])), refs[4]
    plane_ref, off_ref, out_ref, sems = refs[5:]

    def part(p):
        at = pl.ds(2 * p, 2)
        return pltpu.make_async_copy(out_ref.at[at], out_hbm.at[at], sems.at[p])

    coef = coefficients(speeds_ref)
    in_y, _ = rim_coefficients(coef[1], 1)
    in_z, _ = rim_coefficients(coef[2], 2)
    high_y, high_z = bit((8, 128), 1), bit((8, 128), 2)
    some_y, some_z = (2.0 / 3.0) * in_y, (2.0 / 3.0) * in_z
    spread_y, spread_z = spread(coef[1], 1), spread(coef[2], 2)
    weight = (2.0 / 3.0) * weight_ref[...]
    present, share = presence(count_ref)

    planes, limits = [], []
    for p in range(3):
        ends = []
        for n, most in ((0, jnp.maximum), (1, jnp.minimum)):
            y, z = [get_outer(got, axis, EXT[axis] + p, n) for axis in AXES]
            x = most(limit_ref[n, p], most(y, z))
            ends.append(to_rows([(x, x)]))
        limits += list(zip(*ends))
        at = pl.ds(FACE + 2 * p, 2)
        late = weight * jnp.concatenate(
            [get_outer(got, "dev", at, h) for h in range(2)], axis=0
        )
        x = with_faces([late[i] for i in range(4)], local(coef[0], 0))
        at_corner = late + jnp.stack(x) + some_y * corner_ref[0, p]
        to_corner = some_z * corner_ref[1, p]
        both = []
        for k in range(4):
            value = some_y * get_face(got, "dev", p, k, 0) + spread_z[k] * late
            if k in (0, 3):
                value = value + jnp.where(high_z == (k == 3), at_corner, 0.0)
            both.append(value)
        for j in range(4):
            value = some_z * get_face(got, "grp", p, j, 0) + spread_y[j] * late
            if j in (0, 3):
                value = value + jnp.where(high_y == (j == 3), to_corner, 0.0)
            both.append(value)
        planes.append(both)
    for t in range(8):
        for h in range(2):
            rows = to_rows([(planes[p][t][2 * h], planes[p][t][2 * h + 1]) for p in range(3)])
            off = offsets(rows, present, share)
            for f in range(6):
                plane_ref[f, 2 * t + h] = rows[f]
                off_ref[f, 2 * t + h] = off[f]

    rim = rim_ref[...]
    for p in range(3):
        off_high, off_low = split(columns(off_ref, p, 128))
        fix = jnp.dot(rim, jnp.concatenate([off_high, off_low], axis=0), preferred_element_type=jnp.float32)
        fix = fix[:256] + fix[256:]
        for g in range(2):
            f = 2 * p + g
            part_fix = fix[:, 128 * g : 128 * g + 128].reshape(4, 4, 2, 8, 128)
            for k in range(4):
                for j in range(4):
                    at = pl.ds(8 * k + 2 * j, 2)
                    value = base_ref[f, at] + part_fix[k, j]
                    if j in (0, 3):
                        value = value + jnp.where(high_y == (j == 3), plane_ref[f, pl.ds(2 * k, 2)], 0.0)
                    if k in (0, 3):
                        value = value + jnp.where(
                            high_z == (k == 3), plane_ref[f, pl.ds(8 + 2 * j, 2)], 0.0
                        )
                    out_ref[f, at] = jnp.minimum(jnp.maximum(value, limits[f][1]), limits[f][0])
        part(p).start()
    for p in range(3):
        part(p).wait()


def call(kernel, outs, args, scratch=(), flops=5_000_000, space=pltpu.VMEM, out_space=pltpu.VMEM):
    return pl.pallas_call(
        kernel,
        out_shape=[jax.ShapeDtypeStruct(*o) for o in outs],
        in_specs=[pl.BlockSpec(memory_space=space)] * len(args),
        out_specs=[pl.BlockSpec(memory_space=out_space)] * len(outs),
        scratch_shapes=[pltpu.VMEM(*s) if isinstance(s, tuple) else s for s in scratch],
        compiler_params=pltpu.CompilerParams(vmem_limit_bytes=LIMIT),
        cost_estimate=pl.CostEstimate(flops=flops, bytes_accessed=2_000_000, transcendentals=0),
    )(*args)


EVEN_PAIRS = [(i, i ^ 1) for i in range(16)]
ODD_PAIRS = [((i + 1) % 16, ((i ^ 1) + 1) % 16) for i in range(16)]


def exchange(messages, ways):
    pairs = (EVEN_PAIRS, ODD_PAIRS)
    return [lax.ppermute(m, axis, pairs[odd]) for m, (axis, odd) in zip(messages, ways)]


def shards(fields, speeds, sharpen, mat_count):
    f32, bf16 = jnp.float32, jnp.bfloat16
    rows = fields.reshape(ROW)
    speeds = speeds.reshape(24, 128)
    counts = mat_count.reshape(4, 128)
    node, one, ext = (NODE, f32), ((8, 128), f32), ((2, 3, 8, 128), f32)
    corner = ((2, 3, 4, 8, 128), f32)
    q, counts, speeds, *messages = call(
        open_kernel,
        [node, one, ((24, 128), f32)] + [((COEF + 1, 8, 128), f32)] * 4,
        [pltpu.with_memory_space_constraint(x, pltpu.HBM) for x in (rows, speeds, counts)],
        scratch=[(ROW, f32), ((4, 128), jnp.int32), pltpu.SemaphoreType.DMA((5,))],
        space=pltpu.HBM,
    )
    first = exchange(messages, FIRST)
    tall = ((512, 256), bf16)
    base, extremes, both, rim = call(
        local_kernel, [node, ext, tall, tall], [q, speeds, sharpen], scratch=[node]
    )
    s, corners, weight, *messages = call(
        first_kernel,
        [node, corner, one] + [((EXT[axis] + 3, 8, 128), f32) for axis, _ in SECOND],
        [q, base, speeds, extremes, *first],
    )
    second = exchange(messages, SECOND)
    base, limits = call(
        inner_kernel,
        [(ROW, f32), ext],
        [q, s, speeds, extremes, counts, both],
        scratch=[node, (ROW, f32)],
    )
    plane = ((6, 16, 8, 128), f32)
    (out,) = call(
        last_kernel,
        [(ROW, f32)],
        [base, speeds, limits, corners, weight, counts, rim, *second],
        scratch=[plane, plane, (ROW, f32), pltpu.SemaphoreType.DMA((3,))],
        out_space=pltpu.HBM,
    )
    return out.reshape(fields.shape)


def solution(mesh):
    in_specs = (
        P(None, None, "grp", "dev", None),
        P(None, None, "grp", "dev", None),
        P(),
        P("grp", "dev", None),
    )
    out_specs = P(None, None, "grp", "dev", None)
    return jax.shard_map(shards, mesh=mesh, in_specs=in_specs, out_specs=out_specs, check_vma=False)
```

```python
import functools

import jax
import jax.numpy as jnp
import numpy as np
from jax import lax
from jax.experimental import pallas as pl
from jax.experimental.pallas import tpu as pltpu
from jax.sharding import PartitionSpec as P

DT = 0.08
LIFT = 6.0
NODE = (3, 4, 4, 4, 8, 128)
ROW = (6, 32, 8, 128)
FACE = 24
COEF = 2 * FACE
EXT = {"dev": FACE + 6, "grp": FACE}
STEP = {"dev": 1, "grp": 2}
LIMIT = 48 * 1024 * 1024


def gll_derivative():
    points = np.array([-1.0, -1.0 / np.sqrt(5.0), 1.0 / np.sqrt(5.0), 1.0])
    products = np.array(
        [
            np.prod([points[first] - points[second] for second in range(4) if second != first])
            for first in range(4)
        ]
    )
    matrix = np.zeros((4, 4))
    for first in range(4):
        for second in range(4):
            if first != second:
                matrix[first, second] = (
                    products[first] / products[second] / (points[first] - points[second])
                )
        matrix[first, first] = sum(
            (1.0 / (points[first] - points[other]) for other in range(4) if other != first)
        )
    return matrix


D = gll_derivative()
SCALE = [float(x) / 2 for x in (D[0, 0] + D[0, 3], D[0, 0] - D[0, 3], D[0, 1] - D[0, 2])]
RATIO = [float(x) / 2 / s for x, s in zip((D[1, 0] + D[1, 3], D[1, 0] - D[1, 3], D[1, 1] - D[1, 2]), SCALE)]


def roll(x, shift, axis):
    size = x.shape[axis]
    return pltpu.roll(x, shift % size, axis)


def sublane(shape):
    return lax.broadcasted_iota(jnp.int32, shape, len(shape) - 2)


def bit(shape, step):
    return (sublane(shape) & step) != 0


def even_device(axis):
    return lax.rem(lax.axis_index(axis), 2) == 0


def coefficients(speeds_ref, factor=1.0):
    out = []
    low_half = sublane((8, 128)) < 4
    for d in range(3):
        v = speeds_ref[pl.ds(8 * d, 8), :]
        w = roll(v, 4, 0)
        a = jnp.where(low_half, v, w)
        b = jnp.where(low_half, w, v)
        c = 0.5 * (a + b)
        dt = DT * factor
        out.append(
            (
                -dt * c,
                (-dt * LIFT) * (c - jnp.minimum(a, 0.0)),
                (dt * LIFT) * jnp.maximum(a, 0.0),
                (-dt * LIFT) * (jnp.maximum(b, 0.0) - c),
                (-dt * LIFT) * jnp.minimum(b, 0.0),
                (-dt * LIFT) * jnp.minimum(a, 0.0),
                (dt * LIFT) * jnp.maximum(b, 0.0),
            )
        )
    return out


def rim_coefficients(coef, step):
    upper = bit((8, 128), step)
    return jnp.where(upper, coef[4], coef[2]), jnp.where(upper, coef[6], coef[5])


def local(coef, step):
    c, low, low_in, high, high_in = coef[:5]
    if step:
        upper = bit((8, 128), step)
        low_in, high_in = jnp.where(upper, low_in, 0.0), jnp.where(upper, 0.0, high_in)
    return [c * s for s in SCALE], low, low_in, high, high_in, step


def line(q, c):
    t = c[0] * ((q[0] + q[3]) - (q[1] + q[2]))
    o0 = c[1] * (q[0] - q[3])
    o1 = c[2] * (q[1] - q[2])
    e = RATIO[0] * t
    o = RATIO[1] * o0 + RATIO[2] * o1
    o0 = o0 + o1
    return [o0 + t, o + e, o - e, o0 - t]


def beside_faces(q, coef):
    c, low, low_in, high, high_in, step = coef
    axis = q[0].ndim - 2 if step else q[0].ndim - 1
    step = step if step else 1
    r = line(q, c)
    r[0] = r[0] + low_in * roll(q[3], step, axis)
    r[3] = r[3] + high_in * roll(q[0], -step, axis)
    return r


def with_faces(q, coef):
    r = beside_faces(q, coef)
    r[0] = r[0] + coef[1] * q[0]
    r[3] = r[3] + coef[3] * q[3]
    return r


def own_terms(coef, keep):
    x, y, z = [[c[1], 0.0, 0.0, c[3]] for c in coef]
    x = jnp.stack([jnp.broadcast_to(keep + v, (8, 128)) for v in x])
    return [[x + (y[j] + z[k]) for j in range(4)] for k in range(4)]


def beside(low, high, halo_dn, halo_up, step):
    upper = bit(low.shape, step)
    dn = jnp.where(upper, roll(high, step, low.ndim - 2), halo_dn)
    up = jnp.where(upper, halo_up, roll(low, -step, low.ndim - 2))
    return dn, up


def pack_high(a, b, step):
    return jnp.where(bit(a.shape, step), b, roll(a, -step, a.ndim - 2))


def pack_low(a, b, step):
    return jnp.where(bit(a.shape, step), roll(a, step, a.ndim - 2), b)


def unpack_dn(m, second, step):
    return roll(m, -step, m.ndim - 2) if second else m


def unpack_up(m, second, step):
    return roll(m, step, m.ndim - 2) if second else m


def tendency(q_ref, acc_ref, p, along, own, finish, between=lambda step: None):
    for k in range(4):
        between(k)
        rx = beside_faces([q_ref[p, k, :, i] for i in range(4)], along[0])
        for i in range(4):
            acc_ref[p, k, :, i] = rx[i]
        ry = beside_faces([q_ref[p, k, j] for j in range(4)], along[1])
        for j in range(4):
            acc_ref[p, k, j] = acc_ref[p, k, j] + ry[j]
    for j in range(4):
        qz = [q_ref[p, k, j] for k in range(4)]
        rz = beside_faces(qz, along[2])
        for k in range(4):
            finish(p, k, j, acc_ref[p, k, j] + (rz[k] + own[k][j] * qz[k]))


def locals_of(coef):
    return [local(coef[d], d) for d in range(3)]


AXES = ("dev", "grp")
FIRST = (("dev", 1), ("dev", 0), ("grp", 1), ("grp", 0))
SECOND = (("dev", 1), ("dev", 0), ("grp", 1), ("grp", 0))


def put(messages, axis, at, to_next, to_last):
    even = even_device(axis)
    first, second = messages[axis, 0], messages[axis, 1]
    first[at] = jnp.where(even, to_next, to_last)
    second[at] = jnp.where(even, to_last, to_next)


def get_outer(messages, axis, at, second):
    step, even = STEP[axis], even_device(axis)
    first, other = messages[axis, 0][at], messages[axis, 1][at]
    upper = bit(first.shape, step)
    here = upper == even
    if not second:
        return jnp.where(here, first, other)
    there = jnp.where(here, other, first)
    dim = first.ndim - 2
    return jnp.where(upper, roll(there, step, dim), roll(there, -step, dim))


def face(q_ref, p, axis, side, plane):
    return q_ref[p, plane, side] if axis == "dev" else q_ref[p, side, plane]


def put_faces(q_ref, p, messages, base):
    for axis in AXES:
        step = STEP[axis]
        for half in range(2):
            m = 2 * half
            low = [face(q_ref, p, axis, 0, m + h) for h in range(2)]
            high = [face(q_ref, p, axis, 3, m + h) for h in range(2)]
            put(
                messages,
                axis,
                pl.ds(base + 8 * p + 4 * half, 4),
                pack_high(high[0], high[1], step),
                pack_low(low[0], low[1], step),
            )


def get_face(messages, axis, p, plane, base):
    at = pl.ds(base + 8 * p + 4 * (plane // 2), 4)
    return get_outer(messages, axis, at, plane % 2)


def along_plane(h, along_x, along_t):
    out = with_faces(h, along_t)
    for t in range(4):
        out[t] = out[t] + jnp.stack(with_faces([h[t][i] for i in range(4)], along_x))
    return out


def across(coef, step):
    upper = bit((8, 128), step)
    c = jnp.where(upper, -coef[0], coef[0])
    out = [c * float(D[0, n]) for n in range(4)]
    out[0] = out[0] + jnp.where(upper, coef[3], coef[1])
    return out


def put_planes(planes, p, messages, base):
    for axis in AXES:
        step = STEP[axis]
        for half in range(2):
            a, b = planes[axis][2 * half : 2 * half + 2]
            at = pl.ds(base + 8 * p + 4 * half, 4)
            put(messages, axis, at, pack_high(a, b, step), pack_low(a, b, step))


def open_kernel(fields_hbm, speeds_hbm, count_hbm, *refs):
    q_ref, wide_count_ref, speeds_ref = refs[:3]
    messages, (fields_ref, count_ref, sems) = dict(zip(FIRST, refs[3:7])), refs[7:]
    copies = [
        pltpu.make_async_copy(speeds_hbm, speeds_ref, sems.at[3]),
        pltpu.make_async_copy(count_hbm, count_ref, sems.at[4]),
    ]

    def part(p):
        at = pl.ds(2 * p, 2)
        return pltpu.make_async_copy(fields_hbm.at[at], fields_ref.at[at], sems.at[p])

    for copy in copies + [part(p) for p in range(3)]:
        copy.start()
    for copy in copies:
        copy.wait()
    low_half = sublane((8, 128)) < 4
    coef = coefficients(speeds_ref)
    counts = count_ref[...].astype(jnp.float32)
    wide_count_ref[...] = jnp.concatenate([counts, counts], axis=0)
    for axis, d in (("dev", 2), ("grp", 1)):
        pair = rim_coefficients(coef[d], STEP[AXES[d - 1]])
        put(
            messages,
            axis,
            COEF,
            pack_high(pair[0], pair[1], STEP[axis]),
            pack_low(pair[0], pair[1], STEP[axis]),
        )

    along = locals_of(coef)
    across_y, across_z = across(coef[1], 1), across(coef[2], 2)
    high_y, high_z = bit((8, 128), 1), bit((8, 128), 2)

    def pair(p, carry):
        part(p).wait()
        for k in range(4):
            for j in range(4):
                for h in range(2):
                    m = 8 * k + 2 * j + h
                    a = fields_ref[2 * p, m]
                    b = fields_ref[2 * p + 1, m]
                    x = jnp.where(low_half, a, roll(b, 4, 0))
                    y = jnp.where(low_half, roll(a, 4, 0), b)
                    q_ref[p, k, j, 2 * h] = x
                    q_ref[p, k, j, 2 * h + 1] = y
        ys, zs = [], []
        for t in range(4):
            qy, qz = [q_ref[p, t, j] for j in range(4)], [q_ref[p, k, t] for k in range(4)]
            ys.append([jnp.where(high_y, qy[3 - n], qy[n]) for n in range(4)])
            zs.append([jnp.where(high_z, qz[3 - n], qz[n]) for n in range(4)])
        planes = {"dev": [y[0] for y in ys], "grp": [z[0] for z in zs]}
        put_planes(planes, p, messages, 0)
        later = {}
        for axis, lines, ways, other in (("dev", ys, across_y, along[2]), ("grp", zs, across_z, along[1])):
            tangent = along_plane(planes[axis], along[0], other)
            later[axis] = []
            for t in range(4):
                x = ways[0] * lines[t][0] + ways[1] * lines[t][1]
                x = x + (ways[2] * lines[t][2] + ways[3] * lines[t][3])
                later[axis].append(lines[t][0] + (tangent[t] + x))
        put_planes(later, p, messages, FACE)
        return carry

    lax.fori_loop(0, 3, pair, 0)


def bounds(ext_ref, p):
    out = []
    for x, most in ((ext_ref[0, p], jnp.maximum), (ext_ref[1, p], jnp.minimum)):
        y = most(x, most(roll(x, 1, 1), roll(x, -1, 1)))
        for step in (1, 2):
            y = most(y, jnp.where(bit(x.shape, step), roll(x, step, 0), roll(x, -step, 0)))
        out.append(y)
    return out


def spread(coef, step):
    upper = bit((8, 128), step)
    c, low, _, high = coef[:4]
    out = [c * jnp.where(upper, float(D[n, 3]), float(D[n, 0])) for n in range(4)]
    out[0] = out[0] + jnp.where(upper, 0.0, low)
    out[3] = out[3] + jnp.where(upper, high, 0.0)
    return out


def local_kernel(q_ref, speeds_ref, sharpen_ref, out_ref, ext_ref, limit_ref, both_ref, rim_ref, part_ref):
    coef = coefficients(speeds_ref)
    some = coefficients(speeds_ref, 0.25)
    build_operators(sharpen_ref, both_ref, rim_ref)

    own, own_some = own_terms(coef, 1.0), own_terms(some, 0.25)
    along, along_some = locals_of(coef), locals_of(some)

    def middle(p, k, j, t):
        part_ref[p, k, j] = t

    def finish(p, k, j, t):
        out_ref[p, k, j] = 0.75 * q_ref[p, k, j] + t

    def pair(p, carry):
        tops = [q_ref[p, k] for k in range(4)]
        bottoms = tops
        for _ in range(2):
            tops = [jnp.maximum(x, y) for x, y in zip(tops[::2], tops[1::2])]
            bottoms = [jnp.minimum(x, y) for x, y in zip(bottoms[::2], bottoms[1::2])]
        ext_ref[0, p] = jnp.max(tops[0].reshape(16, 8, 128), axis=0)
        ext_ref[1, p] = jnp.min(bottoms[0].reshape(16, 8, 128), axis=0)
        limit_ref[0, p], limit_ref[1, p] = bounds(ext_ref, p)
        tendency(q_ref, part_ref, p, along, own, middle)
        tendency(part_ref, out_ref, p, along_some, own_some, finish)
        return carry

    lax.fori_loop(0, 3, pair, 0)


def first_kernel(q_ref, base_ref, speeds_ref, ext_ref, *refs):
    got, messages = dict(zip(FIRST, refs[:4])), dict(zip(SECOND, refs[7:]))
    out_ref, corner_ref, weight_ref = refs[4:7]
    coef = coefficients(speeds_ref)
    in_y, to_y = rim_coefficients(coef[1], 1)
    in_z, to_z = rim_coefficients(coef[2], 2)
    in_zn, to_zn = [get_outer(got, "dev", COEF, h) for h in range(2)]
    in_ym, to_ym = [get_outer(got, "grp", COEF, h) for h in range(2)]
    weight_ref[...] = 0.25 * (in_y * in_zn + in_z * in_ym)
    weight_n = 0.25 * (to_y * in_z + in_zn * to_ym)
    weight_m = 0.25 * (to_z * in_y + in_ym * to_zn)
    high_y, high_z = bit((8, 128), 1), bit((8, 128), 2)
    some_y, some_z = 0.25 * in_y, 0.25 * in_z
    along = locals_of(coef)
    spread_y, spread_z = spread(coef[1], 1), spread(coef[2], 2)

    def pair(p, carry):
        from_n = [get_face(got, "dev", p, k, 0) for k in range(4)]
        from_m = [get_face(got, "grp", p, j, 0) for j in range(4)]
        edge_n = jnp.where(high_z, from_n[3], from_n[0])
        edge_m = jnp.where(high_y, from_m[3], from_m[0])
        corner_ref[0, p] = weight_n * edge_m
        corner_ref[1, p] = weight_m * edge_n
        put(
            messages,
            "dev",
            pl.ds(FACE + 2 * p, 2),
            pack_high(edge_m[:2], edge_m[2:], 1),
            pack_low(edge_m[:2], edge_m[2:], 1),
        )
        hy = [some_y * x for x in from_n]
        hz = [some_z * x for x in from_m]
        plane_y = along_plane(hy, along[0], along[2])
        plane_z = along_plane(hz, along[0], along[1])
        for n in range(4):
            own = jnp.where(high_y, q_ref[p, n, 3], q_ref[p, n, 0])
            ghost = get_face(got, "dev", p, n, FACE) + to_y * own
            plane_y[n] = plane_y[n] + (hy[n] + some_y * ghost)
            own = jnp.where(high_z, q_ref[p, 3, n], q_ref[p, 0, n])
            ghost = get_face(got, "grp", p, n, FACE) + to_z * own
            plane_z[n] = plane_z[n] + (hz[n] + some_z * ghost)
        for k in range(4):
            for j in range(4):
                value = base_ref[p, k, j] + (spread_y[j] * hy[k] + spread_z[k] * hz[j])
                if j in (0, 3):
                    value = value + jnp.where(high_y == (j == 3), plane_y[k], 0.0)
                if k in (0, 3):
                    value = value + jnp.where(high_z == (k == 3), plane_z[j], 0.0)
                out_ref[p, k, j] = value
        put_faces(out_ref, p, messages, 0)
        for axis in AXES:
            step, pair = STEP[axis], (ext_ref[0, p], ext_ref[1, p])
            put(messages, axis, EXT[axis] + p, pack_high(*pair, step), pack_low(*pair, step))
        return carry

    lax.fori_loop(0, 3, pair, 0)


def build_operators(sharpen_ref, both_ref, rim_ref):
    f32, bf16 = jnp.float32, jnp.bfloat16

    def index(shape, axis):
        return lax.broadcasted_iota(jnp.int32, shape, axis)

    tall = (index((256, 64), 0) // 4 == index((256, 64), 1)).astype(bf16)
    wide = (index((64, 256), 1) // 4 == index((64, 256), 0)).astype(f32)
    node, col = index((64, 128), 0), index((64, 128), 1)
    t, i = (col >> 4) & 3, (col >> 2) & 3
    on_y = 16 * t + 12 * (col & 1) + i
    on_z = 48 * ((col >> 1) & 1) + 4 * t + i
    pick = (node == jnp.where(col < 64, on_y, on_z)).astype(f32)
    wide = jnp.concatenate([wide, pick], axis=1).astype(bf16)
    same = (index((256, 128), 0) & 3) == (index((256, 128), 1) & 3)
    for n, part in enumerate(split(sharpen_ref[...])):
        half = jnp.dot(tall, part, preferred_element_type=f32).astype(bf16)
        full = jnp.dot(half, wide, preferred_element_type=f32)
        full = [jnp.where(same, full[:, 128 * m : 128 * m + 128], 0.0).astype(bf16) for m in range(3)]
        at = pl.ds(256 * n, 256)
        both_ref[at, :] = jnp.concatenate(full[:2], axis=1)
        rim_ref[at, :] = jnp.concatenate([full[2], full[2]], axis=1)


def split(x):
    high = x.astype(jnp.bfloat16)
    return high, (x - high.astype(jnp.float32)).astype(jnp.bfloat16)


def to_rows(pairs):
    low_half = sublane((8, 128)) < 4
    rows = []
    for x, y in pairs:
        rows.append(jnp.where(low_half, x, roll(y, 4, 0)))
        rows.append(jnp.where(low_half, roll(x, 4, 0), y))
    return rows


def presence(count_ref):
    counts = count_ref[...]
    return [(counts > float(f)).astype(jnp.float32) for f in range(6)], 1.0 / counts


def offsets(rows, present, share):
    mean = rows[0] * present[0]
    for f in range(1, 6):
        mean = mean + rows[f] * present[f]
    mean = mean * share
    return [(rows[f] - mean) * present[f] for f in range(6)]


def columns(ref, p, rows):
    return jnp.concatenate([ref[2 * p].reshape(rows, 128), ref[2 * p + 1].reshape(rows, 128)], axis=1)


def inner_kernel(
    q_ref, part_ref, speeds_ref, count_ref, both_ref, out_ref, acc_ref, fix_ref
):
    coef = coefficients(speeds_ref, 2.0 / 3.0)
    low_half = sublane((8, 128)) < 4

    own, along = own_terms(coef, 2.0 / 3.0), locals_of(coef)

    def finish(p, k, j, t):
        acc_ref[p, k, j] = (1.0 / 3.0) * q_ref[p, k, j] + t

    def product(p, step=2):
        if p < 0 or step != 2:
            return
        both = both_ref[...]
        x_high, x_low = parts[p]
        fix = jnp.dot(both, x_high, preferred_element_type=jnp.float32)
        fix = fix[:256] + fix[256:] + jnp.dot(both[:256], x_low, preferred_element_type=jnp.float32)
        for h in range(2):
            fix_ref[2 * p + h] = fix[:, 128 * h : 128 * h + 128].reshape(32, 8, 128)

    parts = []
    for p in range(3):
        tendency(part_ref, acc_ref, p, along, own, finish, functools.partial(product, p - 1))
        for n in range(32):
            k, j, h = n // 8, n // 2 % 4, n % 2
            rows = to_rows([(acc_ref[p, k, j, 2 * h], acc_ref[p, k, j, 2 * h + 1])])
            out_ref[2 * p, n], out_ref[2 * p + 1, n] = rows
        parts.append(split(columns(out_ref, p, 256)))
    product(2)
    present, share = presence(count_ref)
    for n in range(32):
        off = offsets([fix_ref[f, n] for f in range(6)], present, share)
        for f in range(6):
            out_ref[f, n] = out_ref[f, n] + off[f]


def last_kernel(
    base_ref, speeds_ref, limit_ref, corner_ref, weight_ref, count_ref, rim_ref, *refs
):
    got, out_hbm = dict(zip(SECOND, refs[:4])), refs[4]
    plane_ref, off_ref, out_ref, sems = refs[5:]

    def part(p):
        at = pl.ds(2 * p, 2)
        return pltpu.make_async_copy(out_ref.at[at], out_hbm.at[at], sems.at[p])

    coef = coefficients(speeds_ref)
    in_y, _ = rim_coefficients(coef[1], 1)
    in_z, _ = rim_coefficients(coef[2], 2)
    high_y, high_z = bit((8, 128), 1), bit((8, 128), 2)
    some_y, some_z = (2.0 / 3.0) * in_y, (2.0 / 3.0) * in_z
    spread_y, spread_z = spread(coef[1], 1), spread(coef[2], 2)
    weight = (2.0 / 3.0) * weight_ref[...]
    present, share = presence(count_ref)

    planes, limits = [], []
    for p in range(3):
        ends = []
        for n, most in ((0, jnp.maximum), (1, jnp.minimum)):
            y, z = [get_outer(got, axis, EXT[axis] + p, n) for axis in AXES]
            x = most(limit_ref[n, p], most(y, z))
            ends.append(to_rows([(x, x)]))
        limits += list(zip(*ends))
        at = pl.ds(FACE + 2 * p, 2)
        late = weight * jnp.concatenate(
            [get_outer(got, "dev", at, h) for h in range(2)], axis=0
        )
        x = with_faces([late[i] for i in range(4)], local(coef[0], 0))
        at_corner = late + jnp.stack(x) + some_y * corner_ref[0, p]
        to_corner = some_z * corner_ref[1, p]
        both = []
        for k in range(4):
            value = some_y * get_face(got, "dev", p, k, 0) + spread_z[k] * late
            if k in (0, 3):
                value = value + jnp.where(high_z == (k == 3), at_corner, 0.0)
            both.append(value)
        for j in range(4):
            value = some_z * get_face(got, "grp", p, j, 0) + spread_y[j] * late
            if j in (0, 3):
                value = value + jnp.where(high_y == (j == 3), to_corner, 0.0)
            both.append(value)
        planes.append(both)
    for t in range(8):
        for h in range(2):
            rows = to_rows([(planes[p][t][2 * h], planes[p][t][2 * h + 1]) for p in range(3)])
            off = offsets(rows, present, share)
            for f in range(6):
                plane_ref[f, 2 * t + h] = rows[f]
                off_ref[f, 2 * t + h] = off[f]

    rim = rim_ref[...]
    for p in range(3):
        off_high, off_low = split(columns(off_ref, p, 128))
        fix = jnp.dot(rim, jnp.concatenate([off_high, off_low], axis=0), preferred_element_type=jnp.float32)
        fix = fix[:256] + fix[256:]
        for g in range(2):
            f = 2 * p + g
            part_fix = fix[:, 128 * g : 128 * g + 128].reshape(4, 4, 2, 8, 128)
            for k in range(4):
                for j in range(4):
                    at = pl.ds(8 * k + 2 * j, 2)
                    value = base_ref[f, at] + part_fix[k, j]
                    if j in (0, 3):
                        value = value + jnp.where(high_y == (j == 3), plane_ref[f, pl.ds(2 * k, 2)], 0.0)
                    if k in (0, 3):
                        value = value + jnp.where(
                            high_z == (k == 3), plane_ref[f, pl.ds(8 + 2 * j, 2)], 0.0
                        )
                    out_ref[f, at] = jnp.minimum(jnp.maximum(value, limits[f][1]), limits[f][0])
        part(p).start()
    for p in range(3):
        part(p).wait()


def call(kernel, outs, args, scratch=(), flops=5_000_000, space=pltpu.VMEM, out_space=pltpu.VMEM):
    return pl.pallas_call(
        kernel,
        out_shape=[jax.ShapeDtypeStruct(*o) for o in outs],
        in_specs=[pl.BlockSpec(memory_space=space)] * len(args),
        out_specs=[pl.BlockSpec(memory_space=out_space)] * len(outs),
        scratch_shapes=[pltpu.VMEM(*s) if isinstance(s, tuple) else s for s in scratch],
        compiler_params=pltpu.CompilerParams(vmem_limit_bytes=LIMIT),
        cost_estimate=pl.CostEstimate(flops=flops, bytes_accessed=2_000_000, transcendentals=0),
    )(*args)


EVEN_PAIRS = [(i, i ^ 1) for i in range(16)]
ODD_PAIRS = [((i + 1) % 16, ((i ^ 1) + 1) % 16) for i in range(16)]


def exchange(messages, ways):
    pairs = (EVEN_PAIRS, ODD_PAIRS)
    return [lax.ppermute(m, axis, pairs[odd]) for m, (axis, odd) in zip(messages, ways)]


def shards(fields, speeds, sharpen, mat_count):
    f32, bf16 = jnp.float32, jnp.bfloat16
    rows = fields.reshape(ROW)
    speeds = speeds.reshape(24, 128)
    counts = mat_count.reshape(4, 128)
    node, one, ext = (NODE, f32), ((8, 128), f32), ((2, 3, 8, 128), f32)
    corner = ((2, 3, 4, 8, 128), f32)
    q, counts, speeds, *messages = call(
        open_kernel,
        [node, one, ((24, 128), f32)] + [((COEF + 1, 8, 128), f32)] * 4,
        [pltpu.with_memory_space_constraint(x, pltpu.HBM) for x in (rows, speeds, counts)],
        scratch=[(ROW, f32), ((4, 128), jnp.int32), pltpu.SemaphoreType.DMA((5,))],
        space=pltpu.HBM,
    )
    first = exchange(messages, FIRST)
    tall = ((512, 256), bf16)
    base, extremes, limits, both, rim = call(
        local_kernel, [node, ext, ext, tall, tall], [q, speeds, sharpen], scratch=[node]
    )
    s, corners, weight, *messages = call(
        first_kernel,
        [node, corner, one] + [((EXT[axis] + 3, 8, 128), f32) for axis, _ in SECOND],
        [q, base, speeds, extremes, *first],
    )
    second = exchange(messages, SECOND)
    (base,) = call(
        inner_kernel,
        [(ROW, f32)],
        [q, s, speeds, counts, both],
        scratch=[node, (ROW, f32)],
    )
    plane = ((6, 16, 8, 128), f32)
    (out,) = call(
        last_kernel,
        [(ROW, f32)],
        [base, speeds, limits, corners, weight, counts, rim, *second],
        scratch=[plane, plane, (ROW, f32), pltpu.SemaphoreType.DMA((3,))],
        out_space=pltpu.HBM,
    )
    return out.reshape(fields.shape)


def solution(mesh):
    in_specs = (
        P(None, None, "grp", "dev", None),
        P(None, None, "grp", "dev", None),
        P(),
        P("grp", "dev", None),
    )
    out_specs = P(None, None, "grp", "dev", None)
    return jax.shard_map(shards, mesh=mesh, in_specs=in_specs, out_specs=out_specs, check_vma=False)
```

```python
import functools

import jax
import jax.numpy as jnp
import numpy as np
from jax import lax
from jax.experimental import pallas as pl
from jax.experimental.pallas import tpu as pltpu
from jax.sharding import PartitionSpec as P

DT = 0.08
LIFT = 6.0
NODE = (3, 4, 4, 4, 8, 128)
ROW = (6, 32, 8, 128)
FACE = 24
COEF = 2 * FACE
EXT = {"dev": FACE + 6, "grp": FACE}
STEP = {"dev": 1, "grp": 2}
LIMIT = 48 * 1024 * 1024


def gll_derivative():
    points = np.array([-1.0, -1.0 / np.sqrt(5.0), 1.0 / np.sqrt(5.0), 1.0])
    products = np.array(
        [
            np.prod([points[first] - points[second] for second in range(4) if second != first])
            for first in range(4)
        ]
    )
    matrix = np.zeros((4, 4))
    for first in range(4):
        for second in range(4):
            if first != second:
                matrix[first, second] = (
                    products[first] / products[second] / (points[first] - points[second])
                )
        matrix[first, first] = sum(
            (1.0 / (points[first] - points[other]) for other in range(4) if other != first)
        )
    return matrix


D = gll_derivative()
SCALE = [float(x) / 2 for x in (D[0, 0] + D[0, 3], D[0, 0] - D[0, 3], D[0, 1] - D[0, 2])]
RATIO = [float(x) / 2 / s for x, s in zip((D[1, 0] + D[1, 3], D[1, 0] - D[1, 3], D[1, 1] - D[1, 2]), SCALE)]


def roll(x, shift, axis):
    size = x.shape[axis]
    return pltpu.roll(x, shift % size, axis)


def sublane(shape):
    return lax.broadcasted_iota(jnp.int32, shape, len(shape) - 2)


def bit(shape, step):
    return (sublane(shape) & step) != 0


def even_device(axis):
    return lax.rem(lax.axis_index(axis), 2) == 0


def coefficients(speeds_ref, factor=1.0):
    out = []
    low_half = sublane((8, 128)) < 4
    for d in range(3):
        v = speeds_ref[pl.ds(8 * d, 8), :]
        w = roll(v, 4, 0)
        a = jnp.where(low_half, v, w)
        b = jnp.where(low_half, w, v)
        c = 0.5 * (a + b)
        dt = DT * factor
        out.append(
            (
                -dt * c,
                (-dt * LIFT) * (c - jnp.minimum(a, 0.0)),
                (dt * LIFT) * jnp.maximum(a, 0.0),
                (-dt * LIFT) * (jnp.maximum(b, 0.0) - c),
                (-dt * LIFT) * jnp.minimum(b, 0.0),
                (-dt * LIFT) * jnp.minimum(a, 0.0),
                (dt * LIFT) * jnp.maximum(b, 0.0),
            )
        )
    return out


def rim_coefficients(coef, step):
    upper = bit((8, 128), step)
    return jnp.where(upper, coef[4], coef[2]), jnp.where(upper, coef[6], coef[5])


def local(coef, step):
    c, low, low_in, high, high_in = coef[:5]
    if step:
        upper = bit((8, 128), step)
        low_in, high_in = jnp.where(upper, low_in, 0.0), jnp.where(upper, 0.0, high_in)
    return [c * s for s in SCALE], low, low_in, high, high_in, step


def line(q, c):
    t = c[0] * ((q[0] + q[3]) - (q[1] + q[2]))
    o0 = c[1] * (q[0] - q[3])
    o1 = c[2] * (q[1] - q[2])
    e = RATIO[0] * t
    o = RATIO[1] * o0 + RATIO[2] * o1
    o0 = o0 + o1
    return [o0 + t, o + e, o - e, o0 - t]


def beside_faces(q, coef):
    c, low, low_in, high, high_in, step = coef
    axis = q[0].ndim - 2 if step else q[0].ndim - 1
    step = step if step else 1
    r = line(q, c)
    r[0] = r[0] + low_in * roll(q[3], step, axis)
    r[3] = r[3] + high_in * roll(q[0], -step, axis)
    return r


def with_faces(q, coef):
    r = beside_faces(q, coef)
    r[0] = r[0] + coef[1] * q[0]
    r[3] = r[3] + coef[3] * q[3]
    return r


def own_terms(coef, keep):
    x, y, z = [[c[1], 0.0, 0.0, c[3]] for c in coef]
    x = jnp.stack([jnp.broadcast_to(keep + v, (8, 128)) for v in x])
    return [[x + (y[j] + z[k]) for j in range(4)] for k in range(4)]


def beside(low, high, halo_dn, halo_up, step):
    upper = bit(low.shape, step)
    dn = jnp.where(upper, roll(high, step, low.ndim - 2), halo_dn)
    up = jnp.where(upper, halo_up, roll(low, -step, low.ndim - 2))
    return dn, up


def pack_high(a, b, step):
    return jnp.where(bit(a.shape, step), b, roll(a, -step, a.ndim - 2))


def pack_low(a, b, step):
    return jnp.where(bit(a.shape, step), roll(a, step, a.ndim - 2), b)


def unpack_dn(m, second, step):
    return roll(m, -step, m.ndim - 2) if second else m


def unpack_up(m, second, step):
    return roll(m, step, m.ndim - 2) if second else m


def tendency(q_ref, acc_ref, p, along, own, finish, between=lambda step: None):
    for k in range(4):
        between(k)
        rx = beside_faces([q_ref[p, k, :, i] for i in range(4)], along[0])
        for i in range(4):
            acc_ref[p, k, :, i] = rx[i]
        ry = beside_faces([q_ref[p, k, j] for j in range(4)], along[1])
        for j in range(4):
            acc_ref[p, k, j] = acc_ref[p, k, j] + ry[j]
    for j in range(4):
        qz = [q_ref[p, k, j] for k in range(4)]
        rz = beside_faces(qz, along[2])
        for k in range(4):
            finish(p, k, j, acc_ref[p, k, j] + (rz[k] + own[k][j] * qz[k]))


def locals_of(coef):
    return [local(coef[d], d) for d in range(3)]


AXES = ("dev", "grp")
FIRST = (("dev", 1), ("dev", 0), ("grp", 1), ("grp", 0))
SECOND = (("dev", 1), ("dev", 0), ("grp", 1), ("grp", 0))


def put(messages, axis, at, to_next, to_last):
    even = even_device(axis)
    first, second = messages[axis, 0], messages[axis, 1]
    first[at] = jnp.where(even, to_next, to_last)
    second[at] = jnp.where(even, to_last, to_next)


def get_outer(messages, axis, at, second):
    step, even = STEP[axis], even_device(axis)
    first, other = messages[axis, 0][at], messages[axis, 1][at]
    upper = bit(first.shape, step)
    here = upper == even
    if not second:
        return jnp.where(here, first, other)
    there = jnp.where(here, other, first)
    dim = first.ndim - 2
    return jnp.where(upper, roll(there, step, dim), roll(there, -step, dim))


def face(q_ref, p, axis, side, plane):
    return q_ref[p, plane, side] if axis == "dev" else q_ref[p, side, plane]


def put_faces(q_ref, p, messages, base):
    for axis in AXES:
        step = STEP[axis]
        for half in range(2):
            m = 2 * half
            low = [face(q_ref, p, axis, 0, m + h) for h in range(2)]
            high = [face(q_ref, p, axis, 3, m + h) for h in range(2)]
            put(
                messages,
                axis,
                pl.ds(base + 8 * p + 4 * half, 4),
                pack_high(high[0], high[1], step),
                pack_low(low[0], low[1], step),
            )


def get_face(messages, axis, p, plane, base):
    at = pl.ds(base + 8 * p + 4 * (plane // 2), 4)
    return get_outer(messages, axis, at, plane % 2)


def along_plane(h, along_x, along_t):
    out = with_faces(h, along_t)
    for t in range(4):
        out[t] = out[t] + jnp.stack(with_faces([h[t][i] for i in range(4)], along_x))
    return out


def across(coef, step):
    upper = bit((8, 128), step)
    c = jnp.where(upper, -coef[0], coef[0])
    out = [c * float(D[0, n]) for n in range(4)]
    out[0] = out[0] + jnp.where(upper, coef[3], coef[1])
    return out


def put_planes(planes, p, messages, base):
    for axis in AXES:
        step = STEP[axis]
        for half in range(2):
            a, b = planes[axis][2 * half : 2 * half + 2]
            at = pl.ds(base + 8 * p + 4 * half, 4)
            put(messages, axis, at, pack_high(a, b, step), pack_low(a, b, step))


def open_kernel(fields_hbm, speeds_hbm, count_hbm, *refs):
    q_ref, wide_count_ref, speeds_ref = refs[:3]
    messages, (fields_ref, count_ref, sems) = dict(zip(FIRST, refs[3:7])), refs[7:]
    copies = [
        pltpu.make_async_copy(speeds_hbm, speeds_ref, sems.at[3]),
        pltpu.make_async_copy(count_hbm, count_ref, sems.at[4]),
    ]

    def part(p):
        at = pl.ds(2 * p, 2)
        return pltpu.make_async_copy(fields_hbm.at[at], fields_ref.at[at], sems.at[p])

    for copy in copies + [part(p) for p in range(3)]:
        copy.start()
    for copy in copies:
        copy.wait()
    low_half = sublane((8, 128)) < 4
    coef = coefficients(speeds_ref)
    counts = count_ref[...].astype(jnp.float32)
    wide_count_ref[...] = jnp.concatenate([counts, counts], axis=0)
    for axis, d in (("dev", 2), ("grp", 1)):
        pair = rim_coefficients(coef[d], STEP[AXES[d - 1]])
        put(
            messages,
            axis,
            COEF,
            pack_high(pair[0], pair[1], STEP[axis]),
            pack_low(pair[0], pair[1], STEP[axis]),
        )

    along = locals_of(coef)
    across_y, across_z = across(coef[1], 1), across(coef[2], 2)
    high_y, high_z = bit((8, 128), 1), bit((8, 128), 2)

    def pair(p, carry):
        part(p).wait()
        for k in range(4):
            for j in range(4):
                for h in range(2):
                    m = 8 * k + 2 * j + h
                    a = fields_ref[2 * p, m]
                    b = fields_ref[2 * p + 1, m]
                    x = jnp.where(low_half, a, roll(b, 4, 0))
                    y = jnp.where(low_half, roll(a, 4, 0), b)
                    q_ref[p, k, j, 2 * h] = x
                    q_ref[p, k, j, 2 * h + 1] = y
        ys, zs = [], []
        for t in range(4):
            qy, qz = [q_ref[p, t, j] for j in range(4)], [q_ref[p, k, t] for k in range(4)]
            ys.append([jnp.where(high_y, qy[3 - n], qy[n]) for n in range(4)])
            zs.append([jnp.where(high_z, qz[3 - n], qz[n]) for n in range(4)])
        planes = {"dev": [y[0] for y in ys], "grp": [z[0] for z in zs]}
        put_planes(planes, p, messages, 0)
        later = {}
        for axis, lines, ways, other in (("dev", ys, across_y, along[2]), ("grp", zs, across_z, along[1])):
            tangent = along_plane(planes[axis], along[0], other)
            later[axis] = []
            for t in range(4):
                x = ways[0] * lines[t][0] + ways[1] * lines[t][1]
                x = x + (ways[2] * lines[t][2] + ways[3] * lines[t][3])
                later[axis].append(lines[t][0] + (tangent[t] + x))
        put_planes(later, p, messages, FACE)
        return carry

    for p in range(3):
        pair(p, 0)


def bounds(ext_ref, p):
    out = []
    for x, most in ((ext_ref[0, p], jnp.maximum), (ext_ref[1, p], jnp.minimum)):
        y = most(x, most(roll(x, 1, 1), roll(x, -1, 1)))
        for step in (1, 2):
            y = most(y, jnp.where(bit(x.shape, step), roll(x, step, 0), roll(x, -step, 0)))
        out.append(y)
    return out


def spread(coef, step):
    upper = bit((8, 128), step)
    c, low, _, high = coef[:4]
    out = [c * jnp.where(upper, float(D[n, 3]), float(D[n, 0])) for n in range(4)]
    out[0] = out[0] + jnp.where(upper, 0.0, low)
    out[3] = out[3] + jnp.where(upper, high, 0.0)
    return out


def local_kernel(q_ref, speeds_ref, sharpen_ref, out_ref, ext_ref, limit_ref, both_ref, rim_ref, part_ref):
    coef = coefficients(speeds_ref)
    some = coefficients(speeds_ref, 0.25)
    build_operators(sharpen_ref, both_ref, rim_ref)

    own, own_some = own_terms(coef, 1.0), own_terms(some, 0.25)
    along, along_some = locals_of(coef), locals_of(some)

    def middle(p, k, j, t):
        part_ref[p, k, j] = t

    def finish(p, k, j, t):
        out_ref[p, k, j] = 0.75 * q_ref[p, k, j] + t

    def pair(p, carry):
        tops = [q_ref[p, k] for k in range(4)]
        bottoms = tops
        for _ in range(2):
            tops = [jnp.maximum(x, y) for x, y in zip(tops[::2], tops[1::2])]
            bottoms = [jnp.minimum(x, y) for x, y in zip(bottoms[::2], bottoms[1::2])]
        ext_ref[0, p] = jnp.max(tops[0].reshape(16, 8, 128), axis=0)
        ext_ref[1, p] = jnp.min(bottoms[0].reshape(16, 8, 128), axis=0)
        limit_ref[0, p], limit_ref[1, p] = bounds(ext_ref, p)
        tendency(q_ref, part_ref, p, along, own, middle)
        tendency(part_ref, out_ref, p, along_some, own_some, finish)
        return carry

    lax.fori_loop(0, 3, pair, 0)


def first_kernel(q_ref, base_ref, speeds_ref, ext_ref, *refs):
    got, messages = dict(zip(FIRST, refs[:4])), dict(zip(SECOND, refs[7:]))
    out_ref, corner_ref, weight_ref = refs[4:7]
    coef = coefficients(speeds_ref)
    in_y, to_y = rim_coefficients(coef[1], 1)
    in_z, to_z = rim_coefficients(coef[2], 2)
    in_zn, to_zn = [get_outer(got, "dev", COEF, h) for h in range(2)]
    in_ym, to_ym = [get_outer(got, "grp", COEF, h) for h in range(2)]
    weight_ref[...] = 0.25 * (in_y * in_zn + in_z * in_ym)
    weight_n = 0.25 * (to_y * in_z + in_zn * to_ym)
    weight_m = 0.25 * (to_z * in_y + in_ym * to_zn)
    high_y, high_z = bit((8, 128), 1), bit((8, 128), 2)
    some_y, some_z = 0.25 * in_y, 0.25 * in_z
    along = locals_of(coef)
    spread_y, spread_z = spread(coef[1], 1), spread(coef[2], 2)

    def pair(p, carry):
        from_n = [get_face(got, "dev", p, k, 0) for k in range(4)]
        from_m = [get_face(got, "grp", p, j, 0) for j in range(4)]
        edge_n = jnp.where(high_z, from_n[3], from_n[0])
        edge_m = jnp.where(high_y, from_m[3], from_m[0])
        corner_ref[0, p] = weight_n * edge_m
        corner_ref[1, p] = weight_m * edge_n
        put(
            messages,
            "dev",
            pl.ds(FACE + 2 * p, 2),
            pack_high(edge_m[:2], edge_m[2:], 1),
            pack_low(edge_m[:2], edge_m[2:], 1),
        )
        hy = [some_y * x for x in from_n]
        hz = [some_z * x for x in from_m]
        plane_y = along_plane(hy, along[0], along[2])
        plane_z = along_plane(hz, along[0], along[1])
        for n in range(4):
            own = jnp.where(high_y, q_ref[p, n, 3], q_ref[p, n, 0])
            ghost = get_face(got, "dev", p, n, FACE) + to_y * own
            plane_y[n] = plane_y[n] + (hy[n] + some_y * ghost)
            own = jnp.where(high_z, q_ref[p, 3, n], q_ref[p, 0, n])
            ghost = get_face(got, "grp", p, n, FACE) + to_z * own
            plane_z[n] = plane_z[n] + (hz[n] + some_z * ghost)
        for k in range(4):
            for j in range(4):
                value = base_ref[p, k, j] + (spread_y[j] * hy[k] + spread_z[k] * hz[j])
                if j in (0, 3):
                    value = value + jnp.where(high_y == (j == 3), plane_y[k], 0.0)
                if k in (0, 3):
                    value = value + jnp.where(high_z == (k == 3), plane_z[j], 0.0)
                out_ref[p, k, j] = value
        put_faces(out_ref, p, messages, 0)
        for axis in AXES:
            step, pair = STEP[axis], (ext_ref[0, p], ext_ref[1, p])
            put(messages, axis, EXT[axis] + p, pack_high(*pair, step), pack_low(*pair, step))
        return carry

    for p in range(3):
        pair(p, 0)


def build_operators(sharpen_ref, both_ref, rim_ref):
    f32, bf16 = jnp.float32, jnp.bfloat16

    def index(shape, axis):
        return lax.broadcasted_iota(jnp.int32, shape, axis)

    tall = (index((256, 64), 0) // 4 == index((256, 64), 1)).astype(bf16)
    wide = (index((64, 256), 1) // 4 == index((64, 256), 0)).astype(f32)
    node, col = index((64, 128), 0), index((64, 128), 1)
    t, i = (col >> 4) & 3, (col >> 2) & 3
    on_y = 16 * t + 12 * (col & 1) + i
    on_z = 48 * ((col >> 1) & 1) + 4 * t + i
    pick = (node == jnp.where(col < 64, on_y, on_z)).astype(f32)
    wide = jnp.concatenate([wide, pick], axis=1).astype(bf16)
    same = (index((256, 128), 0) & 3) == (index((256, 128), 1) & 3)
    for n, part in enumerate(split(sharpen_ref[...])):
        half = jnp.dot(tall, part, preferred_element_type=f32).astype(bf16)
        full = jnp.dot(half, wide, preferred_element_type=f32)
        full = [jnp.where(same, full[:, 128 * m : 128 * m + 128], 0.0).astype(bf16) for m in range(3)]
        at = pl.ds(256 * n, 256)
        both_ref[at, :] = jnp.concatenate(full[:2], axis=1)
        rim_ref[at, :] = jnp.concatenate([full[2], full[2]], axis=1)


def split(x):
    high = x.astype(jnp.bfloat16)
    return high, (x - high.astype(jnp.float32)).astype(jnp.bfloat16)


def to_rows(pairs):
    low_half = sublane((8, 128)) < 4
    rows = []
    for x, y in pairs:
        rows.append(jnp.where(low_half, x, roll(y, 4, 0)))
        rows.append(jnp.where(low_half, roll(x, 4, 0), y))
    return rows


def presence(count_ref):
    counts = count_ref[...]
    return [(counts > float(f)).astype(jnp.float32) for f in range(6)], 1.0 / counts


def offsets(rows, present, share):
    mean = rows[0] * present[0]
    for f in range(1, 6):
        mean = mean + rows[f] * present[f]
    mean = mean * share
    return [(rows[f] - mean) * present[f] for f in range(6)]


def columns(ref, p, rows):
    return jnp.concatenate([ref[2 * p].reshape(rows, 128), ref[2 * p + 1].reshape(rows, 128)], axis=1)


def inner_kernel(
    q_ref, part_ref, speeds_ref, count_ref, both_ref, out_ref, acc_ref, fix_ref
):
    coef = coefficients(speeds_ref, 2.0 / 3.0)
    low_half = sublane((8, 128)) < 4

    own, along = own_terms(coef, 2.0 / 3.0), locals_of(coef)

    def finish(p, k, j, t):
        acc_ref[p, k, j] = (1.0 / 3.0) * q_ref[p, k, j] + t

    def product(p, step=2):
        if p < 0 or step != 2:
            return
        both = both_ref[...]
        x_high, x_low = parts[p]
        fix = jnp.dot(both, x_high, preferred_element_type=jnp.float32)
        fix = fix[:256] + fix[256:] + jnp.dot(both[:256], x_low, preferred_element_type=jnp.float32)
        for h in range(2):
            fix_ref[2 * p + h] = fix[:, 128 * h : 128 * h + 128].reshape(32, 8, 128)

    parts = []
    for p in range(3):
        tendency(part_ref, acc_ref, p, along, own, finish, functools.partial(product, p - 1))
        for n in range(32):
            k, j, h = n // 8, n // 2 % 4, n % 2
            rows = to_rows([(acc_ref[p, k, j, 2 * h], acc_ref[p, k, j, 2 * h + 1])])
            out_ref[2 * p, n], out_ref[2 * p + 1, n] = rows
        parts.append(split(columns(out_ref, p, 256)))
    product(2)
    present, share = presence(count_ref)
    for n in range(32):
        off = offsets([fix_ref[f, n] for f in range(6)], present, share)
        for f in range(6):
            out_ref[f, n] = out_ref[f, n] + off[f]


def last_kernel(
    base_ref, speeds_ref, limit_ref, corner_ref, weight_ref, count_ref, rim_ref, *refs
):
    got, out_hbm = dict(zip(SECOND, refs[:4])), refs[4]
    plane_ref, off_ref, out_ref, sems = refs[5:]

    def part(p):
        at = pl.ds(2 * p, 2)
        return pltpu.make_async_copy(out_ref.at[at], out_hbm.at[at], sems.at[p])

    coef = coefficients(speeds_ref)
    in_y, _ = rim_coefficients(coef[1], 1)
    in_z, _ = rim_coefficients(coef[2], 2)
    high_y, high_z = bit((8, 128), 1), bit((8, 128), 2)
    some_y, some_z = (2.0 / 3.0) * in_y, (2.0 / 3.0) * in_z
    spread_y, spread_z = spread(coef[1], 1), spread(coef[2], 2)
    weight = (2.0 / 3.0) * weight_ref[...]
    present, share = presence(count_ref)

    planes, limits = [], []
    for p in range(3):
        ends = []
        for n, most in ((0, jnp.maximum), (1, jnp.minimum)):
            y, z = [get_outer(got, axis, EXT[axis] + p, n) for axis in AXES]
            x = most(limit_ref[n, p], most(y, z))
            ends.append(to_rows([(x, x)]))
        limits += list(zip(*ends))
        at = pl.ds(FACE + 2 * p, 2)
        late = weight * jnp.concatenate(
            [get_outer(got, "dev", at, h) for h in range(2)], axis=0
        )
        x = with_faces([late[i] for i in range(4)], local(coef[0], 0))
        at_corner = late + jnp.stack(x) + some_y * corner_ref[0, p]
        to_corner = some_z * corner_ref[1, p]
        both = []
        for k in range(4):
            value = some_y * get_face(got, "dev", p, k, 0) + spread_z[k] * late
            if k in (0, 3):
                value = value + jnp.where(high_z == (k == 3), at_corner, 0.0)
            both.append(value)
        for j in range(4):
            value = some_z * get_face(got, "grp", p, j, 0) + spread_y[j] * late
            if j in (0, 3):
                value = value + jnp.where(high_y == (j == 3), to_corner, 0.0)
            both.append(value)
        planes.append(both)
    for t in range(8):
        for h in range(2):
            rows = to_rows([(planes[p][t][2 * h], planes[p][t][2 * h + 1]) for p in range(3)])
            off = offsets(rows, present, share)
            for f in range(6):
                plane_ref[f, 2 * t + h] = rows[f]
                off_ref[f, 2 * t + h] = off[f]

    rim = rim_ref[...]
    for p in range(3):
        off_high, off_low = split(columns(off_ref, p, 128))
        fix = jnp.dot(rim, jnp.concatenate([off_high, off_low], axis=0), preferred_element_type=jnp.float32)
        fix = fix[:256] + fix[256:]
        for g in range(2):
            f = 2 * p + g
            part_fix = fix[:, 128 * g : 128 * g + 128].reshape(4, 4, 2, 8, 128)
            for k in range(4):
                for j in range(4):
                    at = pl.ds(8 * k + 2 * j, 2)
                    value = base_ref[f, at] + part_fix[k, j]
                    if j in (0, 3):
                        value = value + jnp.where(high_y == (j == 3), plane_ref[f, pl.ds(2 * k, 2)], 0.0)
                    if k in (0, 3):
                        value = value + jnp.where(
                            high_z == (k == 3), plane_ref[f, pl.ds(8 + 2 * j, 2)], 0.0
                        )
                    out_ref[f, at] = jnp.minimum(jnp.maximum(value, limits[f][1]), limits[f][0])
        part(p).start()
    for p in range(3):
        part(p).wait()


def call(kernel, outs, args, scratch=(), flops=5_000_000, space=pltpu.VMEM, out_space=pltpu.VMEM):
    return pl.pallas_call(
        kernel,
        out_shape=[jax.ShapeDtypeStruct(*o) for o in outs],
        in_specs=[pl.BlockSpec(memory_space=space)] * len(args),
        out_specs=[pl.BlockSpec(memory_space=out_space)] * len(outs),
        scratch_shapes=[pltpu.VMEM(*s) if isinstance(s, tuple) else s for s in scratch],
        compiler_params=pltpu.CompilerParams(vmem_limit_bytes=LIMIT),
        cost_estimate=pl.CostEstimate(flops=flops, bytes_accessed=2_000_000, transcendentals=0),
    )(*args)


EVEN_PAIRS = [(i, i ^ 1) for i in range(16)]
ODD_PAIRS = [((i + 1) % 16, ((i ^ 1) + 1) % 16) for i in range(16)]


def exchange(messages, ways):
    pairs = (EVEN_PAIRS, ODD_PAIRS)
    return [lax.ppermute(m, axis, pairs[odd]) for m, (axis, odd) in zip(messages, ways)]


def shards(fields, speeds, sharpen, mat_count):
    f32, bf16 = jnp.float32, jnp.bfloat16
    rows = fields.reshape(ROW)
    speeds = speeds.reshape(24, 128)
    counts = mat_count.reshape(4, 128)
    node, one, ext = (NODE, f32), ((8, 128), f32), ((2, 3, 8, 128), f32)
    corner = ((2, 3, 4, 8, 128), f32)
    q, counts, speeds, *messages = call(
        open_kernel,
        [node, one, ((24, 128), f32)] + [((COEF + 1, 8, 128), f32)] * 4,
        [pltpu.with_memory_space_constraint(x, pltpu.HBM) for x in (rows, speeds, counts)],
        scratch=[(ROW, f32), ((4, 128), jnp.int32), pltpu.SemaphoreType.DMA((5,))],
        space=pltpu.HBM,
    )
    first = exchange(messages, FIRST)
    tall = ((512, 256), bf16)
    base, extremes, limits, both, rim = call(
        local_kernel, [node, ext, ext, tall, tall], [q, speeds, sharpen], scratch=[node]
    )
    s, corners, weight, *messages = call(
        first_kernel,
        [node, corner, one] + [((EXT[axis] + 3, 8, 128), f32) for axis, _ in SECOND],
        [q, base, speeds, extremes, *first],
    )
    second = exchange(messages, SECOND)
    (base,) = call(
        inner_kernel,
        [(ROW, f32)],
        [q, s, speeds, counts, both],
        scratch=[node, (ROW, f32)],
    )
    plane = ((6, 16, 8, 128), f32)
    (out,) = call(
        last_kernel,
        [(ROW, f32)],
        [base, speeds, limits, corners, weight, counts, rim, *second],
        scratch=[plane, plane, (ROW, f32), pltpu.SemaphoreType.DMA((3,))],
        out_space=pltpu.HBM,
    )
    return out.reshape(fields.shape)


def solution(mesh):
    in_specs = (
        P(None, None, "grp", "dev", None),
        P(None, None, "grp", "dev", None),
        P(),
        P("grp", "dev", None),
    )
    out_specs = P(None, None, "grp", "dev", None)
    return jax.shard_map(shards, mesh=mesh, in_specs=in_specs, out_specs=out_specs, check_vma=False)
```
